512 devices in a mesh: band: 32 (over x, y), gate: 16 (over z, core).
Axes of the slice: x: 4, y: 8, z: 8, core: 2. Of those that a mesh axis runs over, the one named last changes fastest.
Arguments:
- messages: bfloat16 [4, 32, 2, 2048, 256], P(None, 'band', None, 'gate'), may hold values from -6 to 6
- gate_type: int32 [4, 32, 2, 2048], P(None, 'band', None, 'gate'), may hold values from 0 to 7
- state_grad: bfloat16 [4, 32, 2, 2048, 256], P(None, 'band', None, 'gate'), may hold values from -6 to 6
- fanin_owner: int32 [4, 32, 2, 2048, 4], P(None, 'band', None, 'gate'), may hold values from 0 to 15, all different within a row; in each aligned block of 128 rows (0 to 127, 128 to 255, ..., all dimensions but the last counted through in order) at most 48 rows name the same one
- fanin_slot: int32 [4, 32, 2, 2048, 4], P(None, 'band', None, 'gate'), may hold values from 0 to 127
- live_count: int32 [4, 32, 2], P(None, 'band'), may hold values from 1024 to 2048, as said below
- hidden_weight: bfloat16 [256, 768], replicated, may hold values from -0.375 to 0.375
- hidden_bias: float32 [768], replicated, may hold values from -3 to 3
- type_table: float32 [8, 768], replicated, may hold values from -6 to 6
Outputs:
- input_grad: bfloat16 [4, 32, 2048, 256], P(None, 'band', 'gate')
- weight_grad: float32 [256, 768], replicated
- bias_grad: float32 [768], replicated
- table_grad: float32 [8, 768], replicated
The draws below stay inside these ranges and needn't reach their ends.
Inputs may be any that keep to these rules, and one draw needn't show every extreme that they name: `fanin_owner`: the 4 fanins of a gate lie on 4 different devices of the gate axis; among the gates of one device (aligned blocks of 128 gates of a level), at most 48 fanins lie on any one device, and exactly 48 on some. `live_count`: gates of a level whose index is below the count are live, the others are padding.
All inputs are finite; a program needn't handle non-finite values.
Results may differ from the reference program's by a relative error of at most 0.0069.
Values may be sent and summed in bfloat16 or wider, within the bound.
A program may use at most 128 MiB of HBM per device.

```python
import math
import jax
import jax.numpy as jnp
import numpy as np
from jax import lax

H = 256
K = 4
TYPES = 8
LEV = 2
M = 4
G_DEV = 128
G_LEV = 2048
BANDS = 32
CAP = 48
N_GATE = 16


def draw_live_count(key, part):
    key = jax.random.fold_in(key, 11)
    counts = jax.random.randint(key, (M, BANDS, LEV), G_LEV // 2, G_LEV + 1, dtype=jnp.int32)
    counts = counts.at[0, 0, 0].set(G_LEV)
    return counts.at[0, BANDS - 1, LEV - 1].set(G_LEV // 2)


def plant(array, key, low, top_value):
    longest = array.shape.index(max(array.shape))
    spots = []
    for shift in (0, 1):
        where = [jax.random.randint(jax.random.fold_in(key, axis), (), 0, length) for axis, length in enumerate(array.shape)]
        where[longest] = (where[longest] + shift) % array.shape[longest]
        spots.append(tuple(where))
    return array.at[spots[0]].set(low).at[spots[1]].set(top_value)


def levels(key, shape, cuts, low, largest):
    loudness, own = 1.0, jax.random.fold_in(key, 6)
    for position, shards_of in cuts:
        heights = jnp.exp(jax.random.uniform(jax.random.fold_in(own, position), (shards_of,), jnp.float32, low / len(cuts), largest / len(cuts)))
        loudness = loudness * jnp.repeat(heights, shape[position] // shards_of).reshape([-1 if axis == position else 1 for axis in range(len(shape))])
    return loudness


def assign_block(key, own, number, rows, amount, top, most, slope):
    sequence = jax.random.permutation(key, amount)
    heavy_load, common = portions_of(amount, rows * top, most, slope, True), portions_of(amount, rows * top, most, slope, False)
    places = jnp.arange(amount)

    def named(lengths, turn):
        used = int((lengths > 0).sum())
        fixed = max(1, used // 4)
        shifted = fixed + (places - fixed + turn * (used - fixed)) % max(1, amount - fixed)
        return jnp.zeros((amount,), jnp.int32).at[sequence[jnp.where(places < fixed, places, shifted)]].set(jnp.asarray(lengths, jnp.int32))

    lengths = jnp.where(number % 4 == 0, named(heavy_load, number // 4), named(common, number - number // 4 - 1))
    mixed = jax.random.permutation(jax.random.fold_in(own, 3), amount)
    giver, sink = mixed[0:amount // 2 * 2:2], mixed[1:amount // 2 * 2:2]
    margin = jnp.minimum(lengths[giver] - 1, most - lengths[sink]) // 2
    margin = jnp.where((giver == sequence[0]) | (sink == sequence[0]) | (lengths[sink] == 0), 0, jnp.maximum(margin, 0))
    shifted = jax.random.randint(jax.random.fold_in(own, 4), (amount // 2,), 0, 1 << 20) % (margin + 1)
    lengths = lengths.at[giver].add(-shifted).at[sink].add(shifted)
    members = jnp.searchsorted(jnp.cumsum(lengths), jnp.arange(rows * top), side="right").astype(jnp.int32)
    table = members.reshape(top, rows).T
    table = table[jax.random.permutation(jax.random.fold_in(own, 1), rows)]
    turn = jax.random.randint(jax.random.fold_in(own, 2), (rows, 1), 0, top)
    return jnp.take_along_axis(table, (jnp.arange(top)[None, :] + turn) % top, axis=1)


def portions_of(number_of, total, limit, skew, full):
    loads = [(1 << 20) // math.isqrt(standing ** skew) + 1 for standing in range(1, number_of + 1)]
    largest = limit if full else min(limit, max(-(-total // number_of), total * loads[0] // sum(loads)))
    least = 1 if total - largest >= number_of - 1 else 0
    given, spare = [largest] + [least] * (number_of - 1), total - largest - least * (number_of - 1)
    while spare > 0:
        movable = [i for i in range(1, number_of) if given[i] < largest] or [i for i in range(1, number_of) if given[i] < limit]
        pool, remaining = sum([loads[i] for i in movable]), spare
        for i in movable:
            extra = min(limit - given[i], max(1, remaining * loads[i] // pool), spare)
            given[i] = given[i] + extra
            spare = spare - extra
    return np.array(given)


def bell_draw(own_key, shape, scale, bound, split=(), held_as=jnp.bfloat16):
    entries = scale * jax.random.normal(own_key, shape, jnp.float32)
    if split:
        entries = entries * levels(own_key, shape, split, -0.22, 0.18)
    return jnp.clip(entries, -bound, bound).astype(held_as)


def setup_inputs(seed: int = 0) -> dict:
    seeds = jax.random.split(jax.random.key(seed), 10)
    messages = bell_draw(seeds[0], (M, BANDS, LEV, G_LEV, H), 1.0, 6.0, ((1, 32), (3, 16)))
    gate_type = plant(jax.random.randint(seeds[1], (M, BANDS, LEV, G_LEV), 0, TYPES), jax.random.fold_in(seeds[1], 1), 0, TYPES - 1).astype(jnp.int32)
    state_grad = bell_draw(seeds[2], (M, BANDS, LEV, G_LEV, H), 1.0, 6.0, ((1, 32), (3, 16)))
    fanin_owner_keys = jax.random.split(jax.random.fold_in(seeds[3], 1), M * BANDS * LEV * G_LEV // G_DEV)
    fanin_owner_turns = jax.random.permutation(jax.random.fold_in(seeds[3], 3), M * BANDS * LEV * G_LEV // G_DEV)
    fanin_owner = jax.vmap(lambda own, number: assign_block(jax.random.fold_in(seeds[3], 2), own, number, G_DEV, N_GATE, K, CAP, 2))(fanin_owner_keys, fanin_owner_turns).reshape((M, BANDS, LEV, G_LEV, K))
    fanin_slot = plant(jax.random.randint(seeds[4], (M, BANDS, LEV, G_LEV, K), 0, G_DEV), jax.random.fold_in(seeds[4], 1), 0, G_DEV - 1).astype(jnp.int32)
    live_count = draw_live_count(jax.random.fold_in(seeds[9], 71), 0)
    hidden_weight = bell_draw(seeds[6], (H, 3 * H), H ** -0.5, 0.375)
    hidden_bias = bell_draw(seeds[7], (3 * H,), 0.5, 3.0, (), jnp.float32)
    type_table = bell_draw(seeds[8], (TYPES, 3 * H), 1.0, 6.0, (), jnp.float32)
    return {"messages": messages, "gate_type": gate_type, "state_grad": state_grad, "fanin_owner": fanin_owner, "fanin_slot": fanin_slot, "live_count": live_count, "hidden_weight": hidden_weight, "hidden_bias": hidden_bias, "type_table": type_table}


def cell_forward(message, kinds, type_rows, weight, bias_row):
    width = message.shape[-1]
    one_hot = (kinds[:, None] == jnp.arange(type_rows.shape[0], dtype=jnp.int32)[None, :]).astype(jnp.float32)
    pre_acts = jnp.dot(message, weight, preferred_element_type=jnp.float32) + bias_row
    inputs = jnp.dot(one_hot, type_rows, precision=lax.Precision.HIGHEST)
    reset_gate = jax.nn.sigmoid(inputs[:, :width] + pre_acts[:, :width])
    update_gate = jax.nn.sigmoid(inputs[:, width:2 * width] + pre_acts[:, width:2 * width])
    candidate = pre_acts[:, 2 * width:]
    new_state = jnp.tanh(inputs[:, 2 * width:] + reset_gate * candidate)
    return (message.astype(jnp.float32), reset_gate, update_gate, candidate, new_state, one_hot)

def cell_backward(cache, state_cot, live, weight):
    message_f, reset_gate, update_gate, candidate, new_state, one_hot = cache
    state_cot = jnp.where(live[:, None], state_cot, 0.0)
    new_pre = state_cot * (1.0 - update_gate) * (1.0 - new_state * new_state)
    reset_pre = new_pre * candidate * reset_gate * (1.0 - reset_gate)
    update_pre = state_cot * (message_f - new_state) * update_gate * (1.0 - update_gate)
    cand_grad = new_pre * reset_gate
    grad_acts = jnp.concatenate([reset_pre, update_pre, cand_grad], axis=1).astype(jnp.bfloat16)
    grad_inputs = jnp.concatenate([grad_acts[:, :2 * reset_pre.shape[1]], new_pre.astype(jnp.bfloat16)], axis=1)
    down_rows = state_cot * update_gate + lax.dot_general(grad_acts, weight, (((1,), (1,)), ((), ())), preferred_element_type=jnp.float32)
    return (grad_acts, grad_inputs, down_rows.astype(jnp.bfloat16))

def band_pass(message, kinds, cotangent, owners, slots, counts, incoming, type_rows, weight, bias_row):
    state_cot = cotangent[LEV - 1].astype(jnp.float32) + incoming
    weight_sum = jnp.zeros((H, 3 * H), jnp.float32)
    bias_sum = jnp.zeros((3 * H,), jnp.float32)
    table_sum = jnp.zeros((TYPES, 3 * H), jnp.float32)
    fanin_grad = jnp.zeros((G_LEV, H), jnp.float32)
    for level in range(LEV - 1, -1, -1):
        cache = cell_forward(message[level], kinds[level], type_rows, weight, bias_row)
        live = jnp.arange(G_LEV, dtype=jnp.int32) < counts[level]
        grad_acts, grad_inputs, down_rows = cell_backward(cache, state_cot, live, weight)
        targets = (owners[level] * G_DEV + slots[level]).reshape(-1).astype(jnp.int32)
        spread = jnp.repeat(down_rows.astype(jnp.float32), K, axis=0)
        fanin_grad = jnp.zeros((G_LEV, H), jnp.float32).at[targets].add(spread)
        weight_sum = weight_sum + lax.dot_general(message[level], grad_acts, (((0,), (0,)), ((), ())), preferred_element_type=jnp.float32)
        bias_sum = bias_sum + lax.optimization_barrier(jnp.sum(grad_acts.astype(jnp.float32), axis=0))
        table_sum = table_sum + lax.dot_general(cache[5], grad_inputs.astype(jnp.float32), (((0,), (0,)), ((), ())), precision=lax.Precision.HIGHEST)
        if level > 0:
            state_cot = cotangent[level - 1].astype(jnp.float32) + fanin_grad
    return (fanin_grad.astype(jnp.bfloat16), weight_sum, bias_sum, table_sum)

def reference(messages, gate_type, state_grad, fanin_owner, fanin_slot, live_count, hidden_weight, hidden_bias, type_table):

    def run_band(pieces):
        return band_pass(*pieces, type_table, hidden_weight, hidden_bias)
    results = []
    weight_total = jnp.zeros((H, 3 * H), jnp.float32)
    bias_total = jnp.zeros((3 * H,), jnp.float32)
    table_total = jnp.zeros((TYPES, 3 * H), jnp.float32)
    for circuit in range(M):
        pieces = (messages[circuit], gate_type[circuit], state_grad[circuit], fanin_owner[circuit], fanin_slot[circuit], live_count[circuit])
        silent = jnp.zeros((BANDS, G_LEV, H), jnp.float32)
        first = lax.map(run_band, pieces + (silent,))[0]
        incoming = jnp.concatenate([first[1:].astype(jnp.float32), jnp.zeros((1, G_LEV, H), jnp.float32)], axis=0)
        final, weight_sum, bias_sum, table_sum = lax.map(run_band, pieces + (incoming,))
        results.append(final)
        weight_total = weight_total + lax.optimization_barrier(jnp.sum(weight_sum, axis=0))
        bias_total = bias_total + lax.optimization_barrier(jnp.sum(bias_sum, axis=0))
        table_total = table_total + lax.optimization_barrier(jnp.sum(table_sum, axis=0))
    scale = 1.0 / math.sqrt(M * BANDS * LEV * G_LEV)
    return (jnp.stack(results), weight_total * scale, bias_total * scale, table_total * scale)
```

```python
import math

import jax
import jax.numpy as jnp
from jax import lax
from jax.experimental import pallas as pl
from jax.experimental.pallas import tpu as pltpu
from jax.sharding import PartitionSpec as P

F32 = jnp.float32
BF16 = jnp.bfloat16
H = 256
ROWS = 128
GATES = 16
CIRC = 4
OWN = 1024
CHUNK = 256
NCH = OWN // CHUNK
SHARE = 896


def iota(shape, dim):
    return lax.broadcasted_iota(jnp.int32, shape, dim)


def dot_tn(a, b):
    return lax.dot_general(a, b, (((0,), (0,)), ((), ())), preferred_element_type=F32)


def dot_nt(a, b):
    return lax.dot_general(a, b, (((1,), (1,)), ((), ())), preferred_element_type=F32)


def dot_nn(a, b):
    return jnp.dot(a, b, preferred_element_type=F32)


def kernel_body(
    bands,
    cols,
    msg,
    types,
    sg,
    owner,
    slot,
    live,
    w,
    bias,
    table,
    out,
    wout,
    eout,
    idx_s,
    idx_r,
    pieces,
    m0,
    sg0,
    m1,
    dm_s,
    d1,
    d2,
    d3,
    d4,
    sel,
    coef,
    xts,
    s0,
    gbuf,
    q_s,
    q_r,
    wacc,
    eacc,
    wsend0,
    wsend1,
    wr0,
    wr1,
    ysend,
    yr,
    xsend,
    xr,
    ag,
    sem_s,
    idx_sem,
    m0_sem,
    sg0_sem,
    dm_sem,
    m1_sem,
    fw_sem,
    ex_sem,
    q_sem,
    out_sem,
    wr_sem,
):
    rows_y = cols
    rows_x = bands // cols
    me = lax.axis_index("gate")
    band = lax.axis_index("band")
    z = me // 2
    half = lax.rem(me, 2)
    active = lax.rem(z, 2) == 0
    mine = z // 2
    sibling = me + 1 - 2 * half
    by = lax.rem(band, rows_y)
    bx = band // rows_y

    def send(src, dst, ssem, rsem, gate=None, to_band=None):
        where = {}
        if to_band is not None:
            where["band"] = to_band
        if gate is not None:
            where["gate"] = gate
        pltpu.make_async_remote_copy(
            src_ref=src,
            dst_ref=dst,
            send_sem=ssem,
            recv_sem=rsem,
            device_id=where,
            device_id_type=pl.DeviceIdType.MESH,
        ).start()

    def wait(ref, sem):
        pltpu.make_async_copy(ref, ref, sem).wait()

    def each(count, body):
        def step(i, carry):
            body(i)
            return carry

        lax.fori_loop(0, count, step, 0)

    barrier = pltpu.get_barrier_semaphore()

    def greet(**where):
        pl.semaphore_signal(
            barrier, inc=1, device_id=where, device_id_type=pl.DeviceIdType.MESH
        )

    each(GATES - 1, lambda i: greet(gate=lax.rem(me + 1 + i, GATES)))
    each(rows_y - 1, lambda i: greet(band=bx * rows_y + lax.rem(by + 1 + i, rows_y)))
    if rows_x > 1:
        each(rows_x - 1, lambda i: greet(band=lax.rem(bx + 1 + i, rows_x) * rows_y + by))
    greet(band=lax.rem(band + 1, bands))
    greet(band=lax.rem(band + bands - 1, bands))

    for c in range(CIRC):
        for lv in range(2):
            idx_s[c, 4 * lv : 4 * lv + 4, :] = owner[c, lv] * ROWS + slot[c, lv]
        idx_s[c, 8:10, :] = types[c]
        idx_s[c, 10:16, :] = jnp.zeros((6, ROWS), jnp.int32)
    full = table[...] + jnp.where(iota((8, 3 * H), 1) < 2 * H, bias[...], 0.0)
    hi = full.astype(BF16)
    rest = full - hi.astype(F32)
    mid = rest.astype(BF16)
    low = (rest - mid.astype(F32)).astype(BF16)
    pieces[...] = jnp.concatenate(
        [hi.astype(F32), mid.astype(F32), low.astype(F32), jnp.zeros((8, 3 * H), F32)], axis=0
    ).astype(BF16)
    cand_bias = bias[:, 2 * H :]

    pl.semaphore_wait(barrier, GATES - 1 + rows_y - 1 + rows_x - 1 + 2)

    def to_task(src_of, dst, ssem, rsem):
        for c in range(CIRC):
            local = jnp.logical_and(active, mine == c)

            @pl.when(local)
            def _():
                dst[...] = src_of(c)[...]

            @pl.when(jnp.logical_not(local))
            def _():
                send(src_of(c), dst, ssem, rsem, gate=4 * c + half)

    for c in range(CIRC):
        for h in range(2):
            local = me == 4 * c + h

            @pl.when(local)
            def _():
                idx_r[me] = idx_s[c]

            @pl.when(jnp.logical_not(local))
            def _():
                send(idx_s.at[c], idx_r.at[me], sem_s.at[0], idx_sem, gate=4 * c + h)

    zrows = pl.ds(pl.multiple_of(z * ROWS, ROWS), ROWS)
    to_task(lambda c: msg.at[c, 0], m0.at[zrows], sem_s.at[1], m0_sem.at[z])
    to_task(lambda c: sg.at[c, 0], sg0.at[zrows], sem_s.at[2], sg0_sem)

    def coefficients(m, kinds, gate0, count):
        hot = jnp.where(lax.bitwise_and(iota((32, ROWS), 0), 7) == kinds, 1.0, 0.0).astype(BF16)
        inp = dot_tn(hot, pieces[...])
        pre = dot_nn(m, w[...])
        tr = jnp.tanh(0.5 * (inp[:, :H] + pre[:, :H]))
        tu = jnp.tanh(0.5 * (inp[:, H : 2 * H] + pre[:, H : 2 * H]))
        cand = pre[:, 2 * H :] + cand_bias
        r = 0.5 + 0.5 * tr
        u = 0.5 + 0.5 * tu
        new = jnp.tanh(inp[:, 2 * H :] + r * cand)
        on = jnp.where(iota((ROWS, 1), 0) + gate0 < count, 1.0, 0.0)
        a = (1.0 - u) * (1.0 - new * new) * on
        dc = a * r
        dr = a * cand * (r * (1.0 - r))
        dz = (m.astype(F32) - new) * (u * (1.0 - u)) * on
        return a, dr, dz, dc, u * on

    def kinds_ext(kinds):
        row = iota((16, ROWS), 0)
        return jnp.where(jnp.logical_or(row == kinds, row == 8), 1.0, 0.0).astype(BF16)

    def grads(s, factors):
        a, b, c, d, u = factors
        dr = (s * b).astype(BF16)
        dz = (s * c).astype(BF16)
        dc = (s * d).astype(BF16)
        dn = (s * a).astype(BF16)
        down = (
            s * u
            + dot_nt(dr, w[:, :H])
            + dot_nt(dz, w[:, H : 2 * H])
            + dot_nt(dc, w[:, 2 * H :])
        )
        return dr, dz, dc, dn, down.astype(BF16)

    wacc[...] = jnp.zeros_like(wacc)
    eacc[...] = jnp.zeros_like(eacc)

    def level_one(c):
        m = msg[c, 1]
        kinds = types[c, 1:2, :]
        factors = coefficients(m, kinds, me * ROWS, live[c, 1])
        dr, dz, dc, dn, down = grads(sg[c, 1].astype(F32), factors)
        dm_s[c] = down
        ext = kinds_ext(kinds)
        for i, g in enumerate((dr, dz, dc)):
            wacc[:, i * H : (i + 1) * H] += dot_tn(m, g)
        for i, g in enumerate((dr, dz, dc, dn)):
            eacc[:, i * H : (i + 1) * H] += dot_nn(ext, g)

    each(CIRC, level_one)

    own_rows = pl.ds(pl.multiple_of(half * OWN + z * ROWS, ROWS), ROWS)
    to_task(lambda c: dm_s.at[c], d1.at[own_rows], sem_s.at[3], dm_sem.at[z])
    to_task(lambda c: msg.at[c, 1], m1.at[zrows], sem_s.at[4], m1_sem.at[z])

    def pack_shares(dst):
        for i in range(GATES):
            dst[i, :, : 3 * H] = wacc[16 * i : 16 * i + 16, :].astype(BF16)
            if i < 8:
                dst[i, :, 3 * H :] = eacc[:, ROWS * i : ROWS * (i + 1)].astype(BF16)
            else:
                dst[i, :, 3 * H :] = jnp.zeros((16, ROWS), BF16)

    def scatter_shares(src, dst, place, ssem, rsem):
        def to(i):
            peer = lax.rem(me + 1 + i, GATES)
            send(src.at[peer], dst.at[place], ssem, rsem, gate=peer)

        each(GATES - 1, to)
        dst[place] = src[me]

    pack_shares(wsend0)
    scatter_shares(wsend0, wr0, me, sem_s.at[5], wr_sem.at[0])

    def turn(t):
        off = jnp.where(lax.rem(t, 2) == 1, (t + 1) // 2, 8 - t // 2)
        return lax.rem(z + off, 8)

    @pl.when(active)
    def _():
        wait(idx_r.at[0 : GATES - 1], idx_sem)

        def build(j):
            tile = idx_r[j]
            col = pl.ds(pl.multiple_of(lax.rem(j, 2) * OWN + (j // 2) * ROWS, ROWS), ROWS)
            spot = iota((ROWS, ROWS), 0)
            block = 2 * iota((8, ROWS), 0) + half
            for lv in (1, 0):
                at = jnp.full((8, ROWS), -1, jnp.int32)
                for f in range(4):
                    t = tile[4 * lv + f : 4 * lv + f + 1, :]
                    at = jnp.where(
                        lax.shift_right_logical(t, 7) == block, lax.bitwise_and(t, 127), at
                    )
                for k in range(8):
                    sel[lv, k * ROWS : (k + 1) * ROWS, col] = jnp.where(
                        spot == at[k : k + 1, :], 1.0, 0.0
                    ).astype(BF16)

        each(GATES, build)

        def forward(lv, m_ref, sem):
            def step(t):
                k = turn(t)

                @pl.when(t > 0)
                def _():
                    wait(m_ref.at[0:ROWS], sem.at[k])

                rows = pl.ds(pl.multiple_of(k * ROWS, ROWS), ROWS)
                j = 2 * k + half
                kinds = idx_r[j, 8 + lv : 9 + lv, :]
                factors = coefficients(m_ref[rows], kinds, j * ROWS, live[mine, lv])
                for i, f in enumerate(factors):
                    coef[lv, i, rows] = f
                xts[lv, :, rows] = kinds_ext(kinds)

            each(8, step)

        forward(0, m0, m0_sem)

        def relay(t):
            k = turn(t)
            rows = pl.ds(pl.multiple_of(half * OWN + k * ROWS, ROWS), ROWS)

            @pl.when(t > 0)
            def _():
                wait(d1.at[0:ROWS], dm_sem.at[k])

            send(d1.at[rows], d1.at[rows], sem_s.at[6], fw_sem, gate=sibling)

        each(8, relay)
        wait(sg0.at[0 : 7 * ROWS], sg0_sem)
        wait(d1.at[0:OWN], fw_sem)

        def chunk(n):
            return pl.ds(pl.multiple_of(n * CHUNK, CHUNK), CHUNK)

        def backward(lv, s, n, dst, sem, ssem):
            rows = chunk(n)
            factors = tuple(coef[lv, i, rows] for i in range(5))
            dr, dz, dc, dn, down = grads(s, factors)
            for i, g in enumerate((dr, dz, dc, dn)):
                gbuf[rows, i * H : (i + 1) * H] = g
            place = pl.ds(pl.multiple_of(half * OWN + n * CHUNK, CHUNK), CHUNK)
            dst[place] = down
            send(dst.at[place], dst.at[place], ssem, sem, gate=sibling)

        def collect(lv, n, src):
            return dot_nn(sel[lv, chunk(n)], src[...])

        def first_zero(n):
            s = sg0[chunk(n)].astype(F32) + collect(1, n, d1)
            s0[chunk(n)] = s
            backward(0, s, n, d2, ex_sem.at[0], sem_s.at[7])

        each(NCH, first_zero)
        wait(d2.at[0:OWN], ex_sem.at[0])

        def first_out(n):
            rows = chunk(n)
            q_s[rows] = collect(0, n, d2).astype(BF16)

            @pl.when(band > 0)
            def _():
                send(
                    q_s.at[rows],
                    q_r.at[rows],
                    sem_s.at[8],
                    q_sem.at[n],
                    to_band=jnp.maximum(band - 1, 0),
                )

            @pl.when(band == bands - 1)
            def _():
                q_r[rows] = jnp.zeros((CHUNK, H), BF16)

        each(NCH, first_out)
        forward(1, m1, m1_sem)

        def second_one(n):
            @pl.when(band < bands - 1)
            def _():
                wait(q_r.at[0:CHUNK], q_sem.at[n])

            backward(1, q_r[chunk(n)].astype(F32), n, d3, ex_sem.at[1], sem_s.at[9])

        each(NCH, second_one)

        for i in range(3):
            wacc[:, i * H : (i + 1) * H] = dot_tn(m1[...], gbuf[:, i * H : (i + 1) * H])
        for i in range(4):
            eacc[:, i * H : (i + 1) * H] = dot_nn(xts[1], gbuf[:, i * H : (i + 1) * H])
        wait(d3.at[0:OWN], ex_sem.at[1])

        def second_zero(n):
            s = s0[chunk(n)] + collect(1, n, d3)
            backward(0, s, n, d4, ex_sem.at[2], sem_s.at[10])

        each(NCH, second_zero)
        for i in range(3):
            wacc[:, i * H : (i + 1) * H] += dot_tn(m0[...], gbuf[:, i * H : (i + 1) * H])
        for i in range(4):
            eacc[:, i * H : (i + 1) * H] += dot_nn(xts[0], gbuf[:, i * H : (i + 1) * H])
        pack_shares(wsend1)
        scatter_shares(wsend1, wr1, 2 * mine + half, sem_s.at[11], wr_sem.at[1])

        wait(d4.at[0:OWN], ex_sem.at[2])

        @pl.when(band > 0)
        def _():
            wait(q_s, sem_s.at[8])

        def second_out(n):
            rows = chunk(n)
            q_s[rows] = collect(0, n, d4).astype(BF16)
            for e in range(2):
                k = 2 * n + e
                part = pl.ds(pl.multiple_of(k * ROWS, ROWS), ROWS)

                @pl.when(k == z)
                def _():
                    out[mine] = q_s[part]

                @pl.when(k != z)
                def _():
                    send(q_s.at[part], out.at[mine], sem_s.at[12], out_sem, gate=2 * k + half)

        each(NCH, second_out)

    wait(wr0.at[0 : GATES - 1], wr_sem.at[0])

    @pl.when(active)
    def _():
        wait(wr1.at[0:7], wr_sem.at[1])

    @pl.when(jnp.logical_not(active))
    def _():
        wait(wr1, wr_sem.at[1])

    total = wr0[0].astype(F32)
    for i in range(1, GATES):
        total = total + wr0[i].astype(F32)
    for i in range(8):
        total = total + wr1[i].astype(F32)
    ysend[...] = total.astype(BF16)

    def to_y(i):
        peer = bx * rows_y + lax.rem(by + 1 + i, rows_y)
        send(ysend, yr.at[by], sem_s.at[13], wr_sem.at[2], to_band=peer)

    each(rows_y - 1, to_y)
    yr[by] = ysend[...]
    wait(yr.at[0 : rows_y - 1], wr_sem.at[2])
    total = yr[0].astype(F32)
    for i in range(1, rows_y):
        total = total + yr[i].astype(F32)
    if rows_x > 1:
        xsend[...] = total.astype(BF16)

        def to_x(i):
            peer = lax.rem(bx + 1 + i, rows_x) * rows_y + by
            send(xsend, xr.at[bx], sem_s.at[14], wr_sem.at[3], to_band=peer)

        each(rows_x - 1, to_x)
        xr[bx] = xsend[...]
        wait(xr.at[0 : rows_x - 1], wr_sem.at[3])
        total = xr[0].astype(F32)
        for i in range(1, rows_x):
            total = total + xr[i].astype(F32)
    total = total * (1.0 / math.sqrt(CIRC * bands * 2 * ROWS * GATES))
    ag[me] = total.astype(BF16)

    def to_all(i):
        peer = lax.rem(me + 1 + i, GATES)
        send(ag.at[me], ag.at[me], sem_s.at[15], wr_sem.at[4], gate=peer)

    each(GATES - 1, to_all)
    wait(ag.at[0 : GATES - 1], wr_sem.at[4])
    for i in range(GATES):
        wout[16 * i : 16 * i + 16, :] = ag[i, :, : 3 * H].astype(F32)
        if i < 8:
            eout[:, ROWS * i : ROWS * (i + 1)] = ag[i, :, 3 * H :].astype(F32)

    @pl.when(active)
    def _():
        wait(out.at[0:3], out_sem)
        wait(idx_r.at[0:7], sem_s.at[0])
        for i in range(1, 5):
            wait(m0.at[0 : 3 * ROWS], sem_s.at[i])
        wait(d1.at[0:OWN], sem_s.at[6])
        wait(d1.at[0:OWN], sem_s.at[7])
        wait(d1.at[0:OWN], sem_s.at[9])
        wait(d1.at[0:OWN], sem_s.at[10])
        wait(wr0.at[0 : GATES - 1], sem_s.at[11])
        wait(q_s.at[0 : 7 * ROWS], sem_s.at[12])

    @pl.when(jnp.logical_not(active))
    def _():
        wait(out, out_sem)
        wait(idx_r.at[0:8], sem_s.at[0])
        for i in range(1, 5):
            wait(m0.at[0 : 4 * ROWS], sem_s.at[i])

    wait(wr0.at[0 : GATES - 1], sem_s.at[5])
    wait(yr.at[0 : rows_y - 1], sem_s.at[13])
    if rows_x > 1:
        wait(xr.at[0 : rows_x - 1], sem_s.at[14])
    wait(ag.at[0 : GATES - 1], sem_s.at[15])


def shards(
    messages,
    gate_type,
    state_grad,
    fanin_owner,
    fanin_slot,
    live_count,
    hidden_weight,
    hidden_bias,
    type_table,
):
    bands = lax.axis_size("band")
    cols = min(8, bands)
    owners = jnp.swapaxes(fanin_owner[:, 0], 2, 3)
    slots = jnp.swapaxes(fanin_slot[:, 0], 2, 3)
    vmem = pl.BlockSpec(memory_space=pltpu.VMEM)
    dma = pltpu.SemaphoreType.DMA

    def body(*refs):
        kernel_body(bands, cols, *refs)

    out, weight, ext = pl.pallas_call(
        body,
        out_shape=(
            jax.ShapeDtypeStruct((CIRC, ROWS, H), BF16),
            jax.ShapeDtypeStruct((H, 3 * H), F32),
            jax.ShapeDtypeStruct((16, 4 * H), F32),
        ),
        in_specs=[vmem] * 5 + [pl.BlockSpec(memory_space=pltpu.SMEM)] + [vmem] * 3,
        out_specs=(vmem, vmem, vmem),
        scratch_shapes=[
            pltpu.VMEM((CIRC, 16, ROWS), jnp.int32),
            pltpu.VMEM((GATES, 16, ROWS), jnp.int32),
            pltpu.VMEM((32, 3 * H), BF16),
            pltpu.VMEM((OWN, H), BF16),
            pltpu.VMEM((OWN, H), BF16),
            pltpu.VMEM((OWN, H), BF16),
            pltpu.VMEM((CIRC, ROWS, H), BF16),
            pltpu.VMEM((2 * OWN, H), BF16),
            pltpu.VMEM((2 * OWN, H), BF16),
            pltpu.VMEM((2 * OWN, H), BF16),
            pltpu.VMEM((2 * OWN, H), BF16),
            pltpu.VMEM((2, OWN, 2 * OWN), BF16),
            pltpu.VMEM((2, 5, OWN, H), F32),
            pltpu.VMEM((2, 16, OWN), BF16),
            pltpu.VMEM((OWN, H), F32),
            pltpu.VMEM((OWN, 4 * H), BF16),
            pltpu.VMEM((OWN, H), BF16),
            pltpu.VMEM((OWN, H), BF16),
            pltpu.VMEM((H, 3 * H), F32),
            pltpu.VMEM((16, 4 * H), F32),
            pltpu.VMEM((GATES, 16, SHARE), BF16),
            pltpu.VMEM((GATES, 16, SHARE), BF16),
            pltpu.VMEM((GATES, 16, SHARE), BF16),
            pltpu.VMEM((8, 16, SHARE), BF16),
            pltpu.VMEM((16, SHARE), BF16),
            pltpu.VMEM((cols, 16, SHARE), BF16),
            pltpu.VMEM((16, SHARE), BF16),
            pltpu.VMEM((max(bands // cols, 1), 16, SHARE), BF16),
            pltpu.VMEM((GATES, 16, SHARE), BF16),
            dma((16,)),
            dma,
            dma((8,)),
            dma,
            dma((8,)),
            dma((8,)),
            dma,
            dma((3,)),
            dma((NCH,)),
            dma,
            dma((5,)),
        ],
        compiler_params=pltpu.CompilerParams(
            collective_id=0, has_side_effects=True, vmem_limit_bytes=56 * 1024 * 1024
        ),
        name="band_passes",
    )(
        messages[:, 0],
        gate_type[:, 0],
        state_grad[:, 0],
        owners,
        slots,
        live_count[:, 0],
        hidden_weight,
        hidden_bias.reshape(1, 3 * H),
        type_table,
    )
    bias = ext[8, : 3 * H]
    rows = jnp.concatenate([ext[:8, : 2 * H], ext[:8, 3 * H :]], axis=1)
    return out[:, None], weight, bias, rows


def solution(mesh):
    return jax.shard_map(
        shards,
        mesh=mesh,
        in_specs=(
            P(None, "band", None, "gate", None),
            P(None, "band", None, "gate"),
            P(None, "band", None, "gate", None),
            P(None, "band", None, "gate", None),
            P(None, "band", None, "gate", None),
            P(None, "band", None),
            P(),
            P(),
            P(),
        ),
        out_specs=(P(None, "band", "gate", None), P(), P(), P()),
        check_vma=False,
    )
```

```python
import math

import jax
import jax.numpy as jnp
from jax import lax
from jax.experimental import pallas as pl
from jax.experimental.pallas import tpu as pltpu
from jax.sharding import PartitionSpec as P

F32 = jnp.float32
BF16 = jnp.bfloat16
H = 256
ROWS = 128
GATES = 16
CIRC = 4
OWN = 1024
CHUNK = 256
NCH = OWN // CHUNK
PIECES = (8, 4, 16, H)


def iota(shape, dim):
    return lax.broadcasted_iota(jnp.int32, shape, dim)


def dot_tn(a, b):
    return lax.dot_general(a, b, (((0,), (0,)), ((), ())), preferred_element_type=F32)


def dot_nt(a, b):
    return lax.dot_general(a, b, (((1,), (1,)), ((), ())), preferred_element_type=F32)


def dot_nn(a, b):
    return jnp.dot(a, b, preferred_element_type=F32)


def kernel_body(
    bands,
    cols,
    msg,
    types,
    sg,
    owner,
    slot,
    live,
    w,
    bias,
    table,
    out,
    summed,
    idx_s,
    idx_r,
    pieces,
    m0,
    sg0,
    m1,
    dm_s,
    d1,
    d2,
    d3,
    d4,
    sel,
    coef,
    xts,
    s0,
    gbuf,
    q_s,
    q_r,
    wacc,
    eacc,
    half_s,
    half_r,
    plane_s,
    plane_r,
    z_r,
    sem_s,
    idx_sem,
    m0_sem,
    sg0_sem,
    dm_sem,
    m1_sem,
    fw_sem,
    ex_sem,
    q_sem,
    out_sem,
    wr_sem,
    plane_ready,
):
    rows_y = cols
    rows_x = bands // cols
    me = lax.axis_index("gate")
    band = lax.axis_index("band")
    z = me // 2
    half = lax.rem(me, 2)
    active = lax.rem(z, 2) == 0
    mine = z // 2
    sibling = me + 1 - 2 * half
    by = lax.rem(band, rows_y)
    bx = band // rows_y

    def send(src, dst, ssem, rsem, gate=None, to_band=None):
        where = {}
        if to_band is not None:
            where["band"] = to_band
        if gate is not None:
            where["gate"] = gate
        pltpu.make_async_remote_copy(
            src_ref=src,
            dst_ref=dst,
            send_sem=ssem,
            recv_sem=rsem,
            device_id=where,
            device_id_type=pl.DeviceIdType.MESH,
        ).start()

    def wait(ref, sem):
        pltpu.make_async_copy(ref, ref, sem).wait()

    def each(count, body):
        def step(i, carry):
            body(i)
            return carry

        lax.fori_loop(0, count, step, 0)

    barrier = pltpu.get_barrier_semaphore()

    def greet(**where):
        pl.semaphore_signal(
            barrier, inc=1, device_id=where, device_id_type=pl.DeviceIdType.MESH
        )

    each(GATES - 1, lambda i: greet(gate=lax.rem(me + 1 + i, GATES)))
    each(rows_y - 1, lambda i: greet(band=bx * rows_y + lax.rem(by + 1 + i, rows_y)))
    if rows_x > 1:
        each(rows_x - 1, lambda i: greet(band=lax.rem(bx + 1 + i, rows_x) * rows_y + by))
    greet(band=lax.rem(band + 1, bands))
    greet(band=lax.rem(band + bands - 1, bands))

    for c in range(CIRC):
        for lv in range(2):
            idx_s[c, 4 * lv : 4 * lv + 4, :] = owner[c, lv] * ROWS + slot[c, lv]
        idx_s[c, 8:10, :] = types[c]
        idx_s[c, 10:16, :] = jnp.zeros((6, ROWS), jnp.int32)
    full_bias = bias[...].reshape(1, 3 * H)
    full = table[...] + jnp.where(iota((8, 3 * H), 1) < 2 * H, full_bias, 0.0)
    hi = full.astype(BF16)
    rest = full - hi.astype(F32)
    mid = rest.astype(BF16)
    low = (rest - mid.astype(F32)).astype(BF16)
    pieces[...] = jnp.concatenate(
        [hi.astype(F32), mid.astype(F32), low.astype(F32), jnp.zeros((8, 3 * H), F32)], axis=0
    ).astype(BF16)
    cand_bias = full_bias[:, 2 * H :]

    def coefficients(m, kinds, gate0, count):
        hot = jnp.where(lax.bitwise_and(iota((32, ROWS), 0), 7) == kinds, 1.0, 0.0).astype(BF16)
        inp = dot_tn(hot, pieces[...])
        pre = dot_nn(m, w[...])
        tr = jnp.tanh(0.5 * (inp[:, :H] + pre[:, :H]))
        tu = jnp.tanh(0.5 * (inp[:, H : 2 * H] + pre[:, H : 2 * H]))
        cand = pre[:, 2 * H :] + cand_bias
        r = 0.5 + 0.5 * tr
        u = 0.5 + 0.5 * tu
        new = jnp.tanh(inp[:, 2 * H :] + r * cand)
        on = jnp.where(iota((ROWS, 1), 0) + gate0 < count, 1.0, 0.0)
        a = (1.0 - u) * (1.0 - new * new) * on
        dc = a * r
        dr = a * cand * (r * (1.0 - r))
        dz = (m.astype(F32) - new) * (u * (1.0 - u)) * on
        return a, dr, dz, dc, u * on

    def kinds_ext(kinds):
        row = iota((16, ROWS), 0)
        return jnp.where(jnp.logical_or(row == kinds, row == 8), 1.0, 0.0).astype(BF16)

    def grads(s, factors):
        a, b, c, d, u = factors
        dr = (s * b).astype(BF16)
        dz = (s * c).astype(BF16)
        dc = (s * d).astype(BF16)
        dn = (s * a).astype(BF16)
        down = (
            s * u
            + dot_nt(dr, w[:, :H])
            + dot_nt(dz, w[:, H : 2 * H])
            + dot_nt(dc, w[:, 2 * H :])
        )
        return dr, dz, dc, dn, down.astype(BF16)

    wacc[...] = jnp.zeros_like(wacc)
    eacc[...] = jnp.zeros_like(eacc)

    def level_one(c):
        m = msg[c, 1]
        kinds = types[c, 1:2, :]
        factors = coefficients(m, kinds, me * ROWS, live[1, c])
        dr, dz, dc, dn, down = grads(sg[c, 1].astype(F32), factors)
        dm_s[c] = down
        ext = kinds_ext(kinds)
        for i, g in enumerate((dr, dz, dc)):
            wacc[:, i * H : (i + 1) * H] += dot_tn(m, g)
        for i, g in enumerate((dr, dz, dc, dn)):
            eacc[:, i * H : (i + 1) * H] += dot_nn(ext, g)

    each(CIRC, level_one)

    pl.semaphore_wait(barrier, GATES - 1 + rows_y - 1 + rows_x - 1 + 2)
    each(
        rows_x - 1,
        lambda i: pl.semaphore_signal(
            plane_ready,
            inc=1,
            device_id={"band": lax.rem(bx + 1 + i, rows_x) * rows_y + by},
            device_id_type=pl.DeviceIdType.MESH,
        ),
    )

    def to_task(src_of, dst, ssem, rsem):
        for c in range(CIRC):
            local = jnp.logical_and(active, mine == c)

            @pl.when(local)
            def _():
                dst[...] = src_of(c)[...]

            @pl.when(jnp.logical_not(local))
            def _():
                send(src_of(c), dst, ssem, rsem, gate=4 * c + half)

    for c in range(CIRC):
        for h in range(2):
            local = me == 4 * c + h

            @pl.when(local)
            def _():
                idx_r[me] = idx_s[c]

            @pl.when(jnp.logical_not(local))
            def _():
                send(idx_s.at[c], idx_r.at[me], sem_s.at[0], idx_sem, gate=4 * c + h)

    zrows = pl.ds(pl.multiple_of(z * ROWS, ROWS), ROWS)
    to_task(lambda c: msg.at[c, 0], m0.at[zrows], sem_s.at[1], m0_sem.at[z])
    to_task(lambda c: sg.at[c, 0], sg0.at[zrows], sem_s.at[2], sg0_sem)

    own_rows = pl.ds(pl.multiple_of(half * OWN + z * ROWS, ROWS), ROWS)
    to_task(lambda c: dm_s.at[c], d1.at[own_rows], sem_s.at[3], dm_sem.at[z])
    py, px = 8 // rows_y, 4 // rows_x

    def piece_of(ref, to):
        return ref.at[pl.ds(lax.rem(to, rows_y) * py, py), pl.ds((to // rows_y) * px, px)]

    def halve(stage, ssem):
        for i in range(GATES):
            for n in range(3):
                half_s[stage, i % 2, i // 2, n] = wacc[
                    16 * i : 16 * i + 16, n * H : (n + 1) * H
                ].astype(BF16)
            if i < 4:
                half_s[stage, i % 2, i // 2, 3] = eacc[:, i * H : (i + 1) * H].astype(BF16)
            else:
                half_s[stage, i % 2, i // 2, 3] = jnp.zeros((16, H), BF16)
        send(
            half_s.at[stage, 1 - half], half_r.at[stage], ssem, wr_sem.at[2 * stage], gate=sibling
        )

    def over_plane(stage, ssem):
        wait(half_r.at[stage], wr_sem.at[2 * stage])
        for p in range(8):
            plane_s[stage, p] = (
                half_s[stage, half, p].astype(F32) + half_r[stage, p].astype(F32)
            ).astype(BF16)

        def to(i):
            peer = lax.rem(band + 1 + i, bands)
            send(
                piece_of(plane_s.at[stage], peer),
                plane_r.at[stage, band],
                ssem,
                wr_sem.at[2 * stage + 1],
                to_band=peer,
            )

        each(bands - 1, to)
        plane_r[stage, band] = piece_of(plane_s.at[stage], band)[...]

    def late():
        to_task(lambda c: msg.at[c, 1], m1.at[zrows], sem_s.at[4], m1_sem.at[z])

    halve(0, sem_s.at[5])

    def turn(t):
        off = jnp.where(lax.rem(t, 2) == 1, (t + 1) // 2, 8 - t // 2)
        return lax.rem(z + off, 8)

    @pl.when(active)
    def _():
        wait(idx_r.at[0 : GATES - 1], idx_sem)

        def build(j):
            tile = idx_r[j]
            col = pl.ds(pl.multiple_of(lax.rem(j, 2) * OWN + (j // 2) * ROWS, ROWS), ROWS)
            spot = iota((ROWS, ROWS), 0)
            block = 2 * iota((8, ROWS), 0) + half
            for lv in (1, 0):
                at = jnp.full((8, ROWS), -1, jnp.int32)
                for f in range(4):
                    t = tile[4 * lv + f : 4 * lv + f + 1, :]
                    at = jnp.where(
                        lax.shift_right_logical(t, 7) == block, lax.bitwise_and(t, 127), at
                    )
                for k in range(8):
                    sel[lv, k * ROWS : (k + 1) * ROWS, col] = jnp.where(
                        spot == at[k : k + 1, :], 1.0, 0.0
                    ).astype(BF16)

        each(GATES, build)
        pl.semaphore_wait(plane_ready, rows_x - 1)
        over_plane(0, sem_s.at[13])

        def forward(lv, m_ref, sem):
            def step(t):
                k = turn(t)

                @pl.when(t > 0)
                def _():
                    wait(m_ref.at[0:ROWS], sem.at[k])

                rows = pl.ds(pl.multiple_of(k * ROWS, ROWS), ROWS)
                j = 2 * k + half
                kinds = idx_r[j, 8 + lv : 9 + lv, :]
                factors = coefficients(m_ref[rows], kinds, j * ROWS, live[lv, mine])
                for i, f in enumerate(factors):
                    coef[lv, i, rows] = f
                xts[lv, :, rows] = kinds_ext(kinds)

            each(8, step)

        forward(0, m0, m0_sem)
        for i in range(1, 4):
            wait(m0.at[0 : 3 * ROWS], sem_s.at[i])
        late()

        def relay(t):
            k = turn(t)
            rows = pl.ds(pl.multiple_of(half * OWN + k * ROWS, ROWS), ROWS)

            @pl.when(t > 0)
            def _():
                wait(d1.at[0:ROWS], dm_sem.at[k])

            send(d1.at[rows], d1.at[rows], sem_s.at[6], fw_sem, gate=sibling)

        each(8, relay)
        wait(sg0.at[0 : 7 * ROWS], sg0_sem)
        wait(d1.at[0:OWN], fw_sem)

        def chunk(n):
            return pl.ds(pl.multiple_of(n * CHUNK, CHUNK), CHUNK)

        def backward(lv, s, n, dst, sem, ssem):
            rows = chunk(n)
            factors = tuple(coef[lv, i, rows] for i in range(5))
            dr, dz, dc, dn, down = grads(s, factors)
            for i, g in enumerate((dr, dz, dc, dn)):
                gbuf[rows, i * H : (i + 1) * H] = g
            place = pl.ds(pl.multiple_of(half * OWN + n * CHUNK, CHUNK), CHUNK)
            dst[place] = down
            send(dst.at[place], dst.at[place], ssem, sem, gate=sibling)

        def collect(lv, n, src):
            return dot_nn(sel[lv, chunk(n)], src[...])

        def first_zero(n):
            s = sg0[chunk(n)].astype(F32) + collect(1, n, d1)
            s0[chunk(n)] = s
            backward(0, s, n, d2, ex_sem.at[0], sem_s.at[7])

        each(NCH, first_zero)
        wait(d2.at[0:OWN], ex_sem.at[0])

        def first_out(n):
            rows = chunk(n)
            q_s[rows] = collect(0, n, d2).astype(BF16)

            @pl.when(jnp.logical_and(band > 0, n < NCH // 2))
            def _():
                send(q_s.at[rows], q_r.at[rows], sem_s.at[8], q_sem.at[n], gate=me + 2)

            @pl.when(jnp.logical_and(band > 0, n >= NCH // 2))
            def _():
                send(
                    q_s.at[rows],
                    q_r.at[rows],
                    sem_s.at[8],
                    q_sem.at[n],
                    to_band=jnp.maximum(band - 1, 0),
                )

            @pl.when(band == bands - 1)
            def _():
                q_r[rows] = jnp.zeros((CHUNK, H), BF16)

        each(NCH, first_out)
        forward(1, m1, m1_sem)

        def second_one(n):
            @pl.when(band < bands - 1)
            def _():
                wait(q_r.at[0:CHUNK], q_sem.at[n])

            backward(1, q_r[chunk(n)].astype(F32), n, d3, ex_sem.at[1], sem_s.at[9])

        each(NCH, second_one)

        for i in range(3):
            wacc[:, i * H : (i + 1) * H] = dot_tn(m1[...], gbuf[:, i * H : (i + 1) * H])
        for i in range(4):
            eacc[:, i * H : (i + 1) * H] = dot_nn(xts[1], gbuf[:, i * H : (i + 1) * H])
        wait(d3.at[0:OWN], ex_sem.at[1])

        def second_zero(n):
            s = s0[chunk(n)] + collect(1, n, d3)
            backward(0, s, n, d4, ex_sem.at[2], sem_s.at[10])

        each(NCH, second_zero)
        for i in range(3):
            wacc[:, i * H : (i + 1) * H] += dot_tn(m0[...], gbuf[:, i * H : (i + 1) * H])
        for i in range(4):
            eacc[:, i * H : (i + 1) * H] += dot_nn(xts[0], gbuf[:, i * H : (i + 1) * H])
        halve(1, sem_s.at[11])

        wait(d4.at[0:OWN], ex_sem.at[2])

        @pl.when(band > 0)
        def _():
            wait(q_s, sem_s.at[8])

        def second_out(n):
            rows = chunk(n)
            q_s[rows] = collect(0, n, d4).astype(BF16)
            for e in range(2):
                k = 2 * n + e
                part = pl.ds(pl.multiple_of(k * ROWS, ROWS), ROWS)

                @pl.when(k == z)
                def _():
                    out[mine] = q_s[part]

                @pl.when(k != z)
                def _():
                    send(q_s.at[part], out.at[mine], sem_s.at[12], out_sem, gate=2 * k + half)

        over_plane(1, sem_s.at[14])
        each(NCH, second_out)

    @pl.when(jnp.logical_not(active))
    def _():
        pl.semaphore_wait(plane_ready, rows_x - 1)
        over_plane(0, sem_s.at[13])
        for i in range(1, 4):
            wait(m0.at[0 : 4 * ROWS], sem_s.at[i])
        late()

        @pl.when(band > 0)
        def _():
            def pass_on(n):
                rows = pl.ds(pl.multiple_of(n * CHUNK, CHUNK), CHUNK)
                wait(q_r.at[0:CHUNK], q_sem.at[n])
                send(
                    q_r.at[rows],
                    q_r.at[rows],
                    sem_s.at[8],
                    q_sem.at[n],
                    gate=me - 2,
                    to_band=jnp.maximum(band - 1, 0),
                )

            each(NCH // 2, pass_on)

    def add_plane(stage):
        total = plane_r[stage, 0].astype(F32)
        for i in range(1, bands):
            total = total + plane_r[stage, i].astype(F32)
        return total

    wait(plane_r.at[0, 0 : bands - 1], wr_sem.at[1])

    @pl.when(active)
    def _():
        wait(plane_r.at[1, 0 : bands - 1], wr_sem.at[3])
        z_r[z] = (add_plane(0) + add_plane(1)).astype(BF16)

    @pl.when(jnp.logical_not(active))
    def _():
        z_r[z] = add_plane(0).astype(BF16)

    def along_z(i):
        peer = 2 * lax.rem(z + 1 + i, 8) + half
        send(z_r.at[z], z_r.at[z], sem_s.at[15], wr_sem.at[4], gate=peer)

    each(7, along_z)
    wait(z_r.at[0:7], wr_sem.at[4])
    total = z_r[0].astype(F32)
    for i in range(1, 8):
        total = total + z_r[i].astype(F32)
    total = total * (1.0 / math.sqrt(CIRC * bands * 2 * ROWS * GATES))
    done = piece_of(summed.at[half], band)
    done[...] = total.astype(BF16)

    def to_plane(i):
        peer = lax.rem(band + 1 + i, bands)
        send(done, done, sem_s.at[16], wr_sem.at[5], to_band=peer)

    each(bands - 1, to_plane)
    wait(plane_r.at[0, 0 : bands - 1], wr_sem.at[5])
    send(summed.at[half], summed.at[half], sem_s.at[17], wr_sem.at[6], gate=sibling)
    wait(summed.at[half], wr_sem.at[6])

    @pl.when(active)
    def _():
        wait(out.at[0:3], out_sem)
        wait(idx_r.at[0:7], sem_s.at[0])
        wait(m0.at[0 : 3 * ROWS], sem_s.at[4])
        wait(d1.at[0:OWN], sem_s.at[6])
        wait(d1.at[0:OWN], sem_s.at[7])
        wait(d1.at[0:OWN], sem_s.at[9])
        wait(d1.at[0:OWN], sem_s.at[10])
        wait(half_r.at[1], sem_s.at[11])
        wait(q_s.at[0 : 7 * ROWS], sem_s.at[12])
        wait(plane_r.at[1, 0 : bands - 1], sem_s.at[14])

    @pl.when(jnp.logical_not(active))
    def _():
        wait(out, out_sem)
        wait(idx_r.at[0:8], sem_s.at[0])
        wait(m0.at[0 : 4 * ROWS], sem_s.at[4])

        @pl.when(band > 0)
        def _():
            wait(q_r.at[0 : OWN // 2], sem_s.at[8])

    wait(half_r.at[0], sem_s.at[5])
    wait(plane_r.at[0, 0 : bands - 1], sem_s.at[13])
    wait(z_r.at[0:7], sem_s.at[15])
    wait(plane_r.at[0, 0 : bands - 1], sem_s.at[16])
    wait(summed.at[half], sem_s.at[17])


def finish_body(moved, summed, out, wout, bout, tout):
    out[...] = moved[...]
    for s in range(GATES):
        for n in range(3):
            wout[16 * s : 16 * s + 16, n * H : (n + 1) * H] = summed[s % 2, s // 2, n].astype(F32)
    for s in range(4):
        ext = summed[s % 2, s // 2, 3].astype(F32)
        if s != 2:
            n = min(s, 2)
            tout[:, n * H : (n + 1) * H] = ext[:8]
        if s < 3:
            bout[s * H : (s + 1) * H] = ext[8]


def shards(
    messages,
    gate_type,
    state_grad,
    fanin_owner,
    fanin_slot,
    live_count,
    hidden_weight,
    hidden_bias,
    type_table,
):
    bands = lax.axis_size("band")
    cols = min(8, bands)
    piece = (8 // cols, 4 // (bands // cols), 16, H)
    owners = jnp.swapaxes(fanin_owner[:, 0], 2, 3)
    slots = jnp.swapaxes(fanin_slot[:, 0], 2, 3)
    vmem = pl.BlockSpec(memory_space=pltpu.VMEM)
    dma = pltpu.SemaphoreType.DMA

    def body(*refs):
        kernel_body(bands, cols, *refs)

    moved, summed = pl.pallas_call(
        body,
        out_shape=(
            jax.ShapeDtypeStruct((CIRC, ROWS, H), BF16),
            jax.ShapeDtypeStruct((2,) + PIECES, BF16),
        ),
        in_specs=[vmem] * 5 + [pl.BlockSpec(memory_space=pltpu.SMEM)] + [vmem] * 3,
        out_specs=(vmem, vmem),
        scratch_shapes=[
            pltpu.VMEM((CIRC, 16, ROWS), jnp.int32),
            pltpu.VMEM((GATES, 16, ROWS), jnp.int32),
            pltpu.VMEM((32, 3 * H), BF16),
            pltpu.VMEM((OWN, H), BF16),
            pltpu.VMEM((OWN, H), BF16),
            pltpu.VMEM((OWN, H), BF16),
            pltpu.VMEM((CIRC, ROWS, H), BF16),
            pltpu.VMEM((2 * OWN, H), BF16),
            pltpu.VMEM((2 * OWN, H), BF16),
            pltpu.VMEM((2 * OWN, H), BF16),
            pltpu.VMEM((2 * OWN, H), BF16),
            pltpu.VMEM((2, OWN, 2 * OWN), BF16),
            pltpu.VMEM((2, 5, OWN, H), F32),
            pltpu.VMEM((2, 16, OWN), BF16),
            pltpu.VMEM((OWN, H), F32),
            pltpu.VMEM((OWN, 4 * H), BF16),
            pltpu.VMEM((OWN, H), BF16),
            pltpu.VMEM((OWN, H), BF16),
            pltpu.VMEM((H, 3 * H), F32),
            pltpu.VMEM((16, 4 * H), F32),
            pltpu.VMEM((2, 2) + PIECES, BF16),
            pltpu.VMEM((2,) + PIECES, BF16),
            pltpu.VMEM((2,) + PIECES, BF16),
            pltpu.VMEM((2, bands) + piece, BF16),
            pltpu.VMEM((8,) + piece, BF16),
            dma((18,)),
            dma,
            dma((8,)),
            dma,
            dma((8,)),
            dma((8,)),
            dma,
            dma((3,)),
            dma((NCH,)),
            dma,
            dma((7,)),
            pltpu.SemaphoreType.REGULAR,
        ],
        compiler_params=pltpu.CompilerParams(
            collective_id=0, has_side_effects=True, vmem_limit_bytes=56 * 1024 * 1024
        ),
        name="band_passes",
    )(
        messages[:, 0],
        gate_type[:, 0],
        state_grad[:, 0],
        owners,
        slots,
        live_count[:, 0].T,
        hidden_weight,
        hidden_bias,
        type_table,
    )
    out, weight, bias, rows = pl.pallas_call(
        finish_body,
        out_shape=(
            jax.ShapeDtypeStruct((CIRC, ROWS, H), BF16),
            jax.ShapeDtypeStruct((H, 3 * H), F32),
            jax.ShapeDtypeStruct((3 * H,), F32),
            jax.ShapeDtypeStruct((8, 3 * H), F32),
        ),
        in_specs=[vmem] * 2,
        out_specs=(vmem,) * 4,
        name="results",
    )(moved, summed)
    return out[:, None], weight, bias, rows


def solution(mesh):
    return jax.shard_map(
        shards,
        mesh=mesh,
        in_specs=(
            P(None, "band", None, "gate", None),
            P(None, "band", None, "gate"),
            P(None, "band", None, "gate", None),
            P(None, "band", None, "gate", None),
            P(None, "band", None, "gate", None),
            P(None, "band", None),
            P(),
            P(),
            P(),
        ),
        out_specs=(P(None, "band", "gate", None), P(), P(), P()),
        check_vma=False,
    )
```

```python
import math

import jax
import jax.numpy as jnp
from jax import lax
from jax.experimental import pallas as pl
from jax.experimental.pallas import tpu as pltpu
from jax.sharding import PartitionSpec as P

F32 = jnp.float32
BF16 = jnp.bfloat16
H = 256
ROWS = 128
GATES = 16
CIRC = 4
OWN = 1024
CHUNK = 256
NCH = OWN // CHUNK
PART = 64
PASSED = 5 * ROWS // 2
DETOUR = 384
PIECES = (8, 4, 16, H)


def iota(shape, dim):
    return lax.broadcasted_iota(jnp.int32, shape, dim)


def dot_tn(a, b):
    return lax.dot_general(a, b, (((0,), (0,)), ((), ())), preferred_element_type=F32)


def dot_nt(a, b):
    return lax.dot_general(a, b, (((1,), (1,)), ((), ())), preferred_element_type=F32)


def dot_nn(a, b):
    return jnp.dot(a, b, preferred_element_type=F32)


def kernel_body(
    bands,
    cols,
    msg,
    types,
    sg,
    owner,
    slot,
    live,
    w,
    bias,
    table,
    out,
    summed,
    idx_s,
    idx_r,
    pieces,
    m0,
    sg0,
    m1,
    dm_s,
    d1,
    d2,
    d3,
    d4,
    sel,
    coef,
    xts,
    s0,
    gbuf,
    q_s,
    q_r,
    wacc,
    eacc,
    half_s,
    half_r,
    plane_s,
    plane_r,
    plane_t,
    z_r,
    sem_s,
    idx_sem,
    fi_sem,
    m0_sem,
    sg0_sem,
    dm_sem,
    m1_sem,
    fw_sem,
    ex_sem,
    q_sem,
    qp_sem,
    out_sem,
    wr_sem,
    plane_ready,
    pair_ready,
    below_ready,
):
    rows_y = cols
    rows_x = bands // cols
    me = lax.axis_index("gate")
    band = lax.axis_index("band")
    z = me // 2
    half = lax.rem(me, 2)
    mine = z // 2
    sibling = me + 1 - 2 * half
    by = lax.rem(band, rows_y)
    bx = band // rows_y

    def parity_of(b):
        return lax.rem(b + b // rows_y, 2)

    parity = parity_of(band)
    active = lax.rem(z, 2) == parity
    below = jnp.maximum(band - 1, 0)
    below_parity = parity_of(below)
    beside_y = bx * rows_y + by + 1 - 2 * lax.rem(by, 2)
    beside_x = (bx + 1 - 2 * lax.rem(bx, 2)) * rows_y + by if rows_x > 1 else beside_y

    def send(src, dst, ssem, rsem, gate=None, to_band=None):
        where = {}
        if to_band is not None:
            where["band"] = to_band
        if gate is not None:
            where["gate"] = gate
        pltpu.make_async_remote_copy(
            src_ref=src,
            dst_ref=dst,
            send_sem=ssem,
            recv_sem=rsem,
            device_id=where,
            device_id_type=pl.DeviceIdType.MESH,
        ).start()

    def wait(ref, sem):
        pltpu.make_async_copy(ref, ref, sem).wait()

    def each(count, body):
        def step(i, carry):
            body(i)
            return carry

        lax.fori_loop(0, count, step, 0)

    barrier = pltpu.get_barrier_semaphore()

    def greet(**where):
        pl.semaphore_signal(
            barrier, inc=1, device_id=where, device_id_type=pl.DeviceIdType.MESH
        )

    each(GATES - 1, lambda i: greet(gate=lax.rem(me + 1 + i, GATES)))
    each(rows_y - 1, lambda i: greet(band=bx * rows_y + lax.rem(by + 1 + i, rows_y)))
    if rows_x > 1:
        each(rows_x - 1, lambda i: greet(band=lax.rem(bx + 1 + i, rows_x) * rows_y + by))
    greet(band=lax.rem(band + 1, bands))
    greet(band=lax.rem(band + bands - 1, bands))

    for c in range(CIRC):
        for lv in range(2):
            idx_s[c, 4 * lv : 4 * lv + 4, :] = owner[c, lv] * ROWS + slot[c, lv]
        idx_s[c, 8:10, :] = types[c]
        idx_s[c, 10:16, :] = jnp.zeros((6, ROWS), jnp.int32)
    full_bias = bias[...].reshape(1, 3 * H)
    full = table[...] + jnp.where(iota((8, 3 * H), 1) < 2 * H, full_bias, 0.0)
    hi = full.astype(BF16)
    rest = full - hi.astype(F32)
    mid = rest.astype(BF16)
    low = (rest - mid.astype(F32)).astype(BF16)
    pieces[...] = jnp.concatenate(
        [hi.astype(F32), mid.astype(F32), low.astype(F32), jnp.zeros((8, 3 * H), F32)], axis=0
    ).astype(BF16)
    cand_bias = full_bias[:, 2 * H :]

    def coefficients(m, kinds, gate0, count):
        hot = jnp.where(lax.bitwise_and(iota((32, ROWS), 0), 7) == kinds, 1.0, 0.0).astype(BF16)
        inp = dot_tn(hot, pieces[...])
        pre = dot_nn(m, w[...])
        tr = jnp.tanh(0.5 * (inp[:, :H] + pre[:, :H]))
        tu = jnp.tanh(0.5 * (inp[:, H : 2 * H] + pre[:, H : 2 * H]))
        cand = pre[:, 2 * H :] + cand_bias
        r = 0.5 + 0.5 * tr
        u = 0.5 + 0.5 * tu
        new = jnp.tanh(inp[:, 2 * H :] + r * cand)
        on = jnp.where(iota((ROWS, 1), 0) + gate0 < count, 1.0, 0.0)
        a = (1.0 - u) * (1.0 - new * new) * on
        dc = a * r
        dr = a * cand * (r * (1.0 - r))
        dz = (m.astype(F32) - new) * (u * (1.0 - u)) * on
        return a, dr, dz, dc, u * on

    def kinds_ext(kinds):
        row = iota((16, ROWS), 0)
        return jnp.where(jnp.logical_or(row == kinds, row == 8), 1.0, 0.0).astype(BF16)

    def grads(s, factors):
        a, b, c, d, u = factors
        dr = (s * b).astype(BF16)
        dz = (s * c).astype(BF16)
        dc = (s * d).astype(BF16)
        dn = (s * a).astype(BF16)
        down = (
            s * u
            + dot_nt(dr, w[:, :H])
            + dot_nt(dz, w[:, H : 2 * H])
            + dot_nt(dc, w[:, 2 * H :])
        )
        return dr, dz, dc, dn, down.astype(BF16)

    wacc[...] = jnp.zeros_like(wacc)
    eacc[...] = jnp.zeros_like(eacc)

    def level_one(c):
        m = msg[c, 1]
        kinds = types[c, 1:2, :]
        factors = coefficients(m, kinds, me * ROWS, live[1, c])
        dr, dz, dc, dn, down = grads(sg[c, 1].astype(F32), factors)
        dm_s[c] = down
        ext = kinds_ext(kinds)
        for i, g in enumerate((dr, dz, dc)):
            wacc[:, i * H : (i + 1) * H] += dot_tn(m, g)
        for i, g in enumerate((dr, dz, dc, dn)):
            eacc[:, i * H : (i + 1) * H] += dot_nn(ext, g)

    each(CIRC, level_one)

    pl.semaphore_wait(barrier, GATES - 1 + rows_y - 1 + rows_x - 1 + 2)
    each(
        rows_x - 1,
        lambda i: pl.semaphore_signal(
            plane_ready,
            inc=1,
            device_id={"band": lax.rem(bx + 1 + i, rows_x) * rows_y + by},
            device_id_type=pl.DeviceIdType.MESH,
        ),
    )
    for b in (beside_y, beside_x)[: min(rows_x, 2)]:
        pl.semaphore_signal(
            pair_ready, inc=1, device_id={"band": b}, device_id_type=pl.DeviceIdType.MESH
        )

    @pl.when(band < bands - 1)
    def _():
        pl.semaphore_signal(
            below_ready,
            inc=1,
            device_id={"band": jnp.minimum(band + 1, bands - 1)},
            device_id_type=pl.DeviceIdType.MESH,
        )

    def block(k):
        return pl.ds(pl.multiple_of(k * ROWS, ROWS), ROWS)

    def half_block(k, e):
        return pl.ds(pl.multiple_of(k * ROWS + e * (ROWS // 2), ROWS // 2), ROWS // 2)

    def steps_to(c):
        return lax.rem(2 * c + parity + 8 - z, 8)

    def gate_of(c):
        return 2 * (2 * c + parity) + half

    top, bottom = pl.ds(0, ROWS // 2), pl.ds(ROWS // 2, ROWS // 2)

    def to_task(src_of, buf, base, ssem, rsem):
        for c in range(CIRC):
            steps = steps_to(c)

            @pl.when(steps == 0)
            def _():
                buf[block(base + z)] = src_of(c)[...]

            @pl.when(steps == 4)
            def _():
                send(
                    src_of(c).at[top],
                    buf.at[half_block(base + z, 0)],
                    ssem,
                    rsem.at[z],
                    gate=gate_of(c),
                )

            @pl.when(
                jnp.logical_and(
                    jnp.logical_and(steps != 0, steps != 4),
                    jnp.logical_and(steps != 1, steps != 7),
                )
            )
            def _():
                send(src_of(c), buf.at[block(base + z)], ssem, rsem.at[z], gate=gate_of(c))

    def to_task_by(src_of, buf, base, ssem, rsem):
        for c in range(CIRC):
            steps = steps_to(c)

            @pl.when(steps == 1)
            def _():
                send(
                    src_of(c),
                    buf.at[block(base + z)],
                    ssem,
                    rsem.at[z],
                    gate=gate_of(c),
                    to_band=beside_y,
                )

            @pl.when(steps == 4)
            def _():
                send(
                    src_of(c).at[bottom],
                    buf.at[half_block(base + z, 1)],
                    ssem,
                    rsem.at[z],
                    gate=gate_of(c),
                    to_band=beside_y,
                )

            @pl.when(steps == 7)
            def _():
                send(
                    src_of(c),
                    buf.at[block(base + z)],
                    ssem,
                    rsem.at[z],
                    gate=gate_of(c),
                    to_band=beside_x,
                )

    def hand_on(buf, base, ssem, rsem):
        for steps, b in ((1, beside_y), (7, beside_x), (4, beside_y)):
            k = lax.rem(z + 8 - steps, 8)
            place = half_block(base + k, 1) if steps == 4 else block(base + k)
            wait(buf.at[0 : ROWS // 2] if steps == 4 else buf.at[0:ROWS], rsem.at[k])
            send(buf.at[place], buf.at[place], ssem, rsem.at[k], to_band=b)

    for c in range(CIRC):

        @pl.when(steps_to(c) == 0)
        def _():
            idx_r[half, z] = idx_s[c]

        @pl.when(steps_to(c) != 0)
        def _():
            send(idx_s.at[c], idx_r.at[half, z], sem_s.at[0], idx_sem, gate=gate_of(c))

    first_units = (
        (lambda c: msg.at[c, 0], m0, 0, sem_s.at[1], m0_sem),
        (lambda c: sg.at[c, 0], sg0, 0, sem_s.at[2], sg0_sem),
        (lambda c: dm_s.at[c], d1, 8 * half, sem_s.at[3], dm_sem),
    )
    last_unit = (lambda c: msg.at[c, 1], m1, 0, sem_s.at[4], m1_sem)
    for unit in first_units:
        to_task(*unit)
    pl.semaphore_wait(pair_ready, min(rows_x, 2))
    for unit in first_units:
        to_task_by(*unit)
    py, px = 8 // rows_y, 4 // rows_x

    def piece_of(ref, to):
        return ref.at[pl.ds(lax.rem(to, rows_y) * py, py), pl.ds((to // rows_y) * px, px)]

    def halve(stage, ssem):
        for i in range(GATES):
            for n in range(3):
                half_s[stage, i % 2, i // 2, n] = wacc[
                    16 * i : 16 * i + 16, n * H : (n + 1) * H
                ].astype(BF16)
            if i < 4:
                half_s[stage, i % 2, i // 2, 3] = eacc[:, i * H : (i + 1) * H].astype(BF16)
            else:
                half_s[stage, i % 2, i // 2, 3] = jnp.zeros((16, H), BF16)
        send(
            half_s.at[stage, 1 - half], half_r.at[stage], ssem, wr_sem.at[2 * stage], gate=sibling
        )

    def over_plane(stage, dst, ssem):
        wait(half_r.at[stage], wr_sem.at[2 * stage])
        for p in range(8):
            plane_s[stage, p] = (
                half_s[stage, half, p].astype(F32) + half_r[stage, p].astype(F32)
            ).astype(BF16)

        def to(i):
            peer = lax.rem(band + 1 + i, bands)
            send(
                piece_of(plane_s.at[stage], peer),
                dst,
                ssem,
                wr_sem.at[2 * stage + 1],
                to_band=peer,
            )

        each(bands - 1, to)
        dst[...] = piece_of(plane_s.at[stage], band)[...]

    def late():
        to_task(*last_unit)
        to_task_by(*last_unit)

    halve(0, sem_s.at[5])

    def turn(t):
        off = jnp.where(lax.rem(t, 2) == 1, (t + 1) // 2, 8 - t // 2)
        return lax.rem(z + off, 8)

    @pl.when(active)
    def _():
        wait(idx_r.at[0, 0:7], idx_sem)
        send(idx_r.at[half], idx_r.at[half], sem_s.at[18], fi_sem, gate=sibling)

        def build(j):
            tile = idx_r[j // 8, lax.rem(j, 8)]
            col = pl.ds(pl.multiple_of(j * ROWS, ROWS), ROWS)
            spot = iota((ROWS, ROWS), 0)
            block = 2 * iota((8, ROWS), 0) + half
            for lv in (1, 0):
                at = jnp.full((8, ROWS), -1, jnp.int32)
                for f in range(4):
                    t = tile[4 * lv + f : 4 * lv + f + 1, :]
                    at = jnp.where(
                        lax.shift_right_logical(t, 7) == block, lax.bitwise_and(t, 127), at
                    )
                for k in range(8):
                    sel[lv, k * ROWS : (k + 1) * ROWS, col] = jnp.where(
                        spot == at[k : k + 1, :], 1.0, 0.0
                    ).astype(BF16)

        each(8, lambda k: build(8 * half + k))
        wait(idx_r.at[0], fi_sem)
        each(8, lambda k: build(8 - 8 * half + k))
        pl.semaphore_wait(plane_ready, rows_x - 1)
        over_plane(0, plane_r.at[band], sem_s.at[13])

        def forward(lv, m_ref, sem):
            def step(t):
                k = turn(t)

                @pl.when(t > 0)
                def _():
                    wait(m_ref.at[0:ROWS], sem.at[k])

                rows = pl.ds(pl.multiple_of(k * ROWS, ROWS), ROWS)
                j = 2 * k + half
                kinds = idx_r[half, k, 8 + lv : 9 + lv, :]
                factors = coefficients(m_ref[rows], kinds, j * ROWS, live[lv, mine])
                for i, f in enumerate(factors):
                    coef[lv, i, rows] = f
                xts[lv, :, rows] = kinds_ext(kinds)

            each(8, step)

        forward(0, m0, m0_sem)
        for i in range(1, 4):
            wait(m0.at[0 : 3 * ROWS], sem_s.at[i])
        late()

        def relay(t):
            k = turn(t)
            rows = pl.ds(pl.multiple_of(half * OWN + k * ROWS, ROWS), ROWS)

            @pl.when(t > 0)
            def _():
                wait(d1.at[0:ROWS], dm_sem.at[k])

            send(d1.at[rows], d1.at[rows], sem_s.at[6], fw_sem, gate=sibling)

        each(8, relay)
        each(7, lambda i: wait(sg0.at[0:ROWS], sg0_sem.at[lax.rem(z + 1 + i, 8)]))
        wait(d1.at[0:OWN], fw_sem)

        def chunk(n):
            return pl.ds(pl.multiple_of(n * CHUNK, CHUNK), CHUNK)

        def backward(lv, s, n, dst, sem, ssem):
            rows = chunk(n)
            factors = tuple(coef[lv, i, rows] for i in range(5))
            dr, dz, dc, dn, down = grads(s, factors)
            for i, g in enumerate((dr, dz, dc, dn)):
                gbuf[rows, i * H : (i + 1) * H] = g
            place = pl.ds(pl.multiple_of(half * OWN + n * CHUNK, CHUNK), CHUNK)
            dst[place] = down
            send(dst.at[place], dst.at[place], ssem, sem, gate=sibling)

        def collect(lv, n, src):
            return dot_nn(sel[lv, chunk(n)], src[...])

        @pl.when(band > 0)
        def _():
            pl.semaphore_wait(below_ready, 1)

        def first_zero(n):
            s = sg0[chunk(n)].astype(F32) + collect(1, n, d1)
            s0[chunk(n)] = s
            backward(0, s, n, d2, ex_sem.at[0], sem_s.at[7])

        each(NCH, first_zero)
        wait(d2.at[0:OWN], ex_sem.at[0])

        def first_out(n):
            rows = chunk(n)
            q_s[rows] = collect(0, n, d2).astype(BF16)

            @pl.when(band > 0)
            def _():
                def part(e):
                    i = n * (CHUNK // PART) + e
                    place = pl.ds(pl.multiple_of(i * PART, PART), PART)

                    @pl.when(i < DETOUR // PART)
                    def _():
                        send(
                            q_s.at[place],
                            q_r.at[place],
                            sem_s.at[8],
                            qp_sem.at[i],
                            gate=2 * (2 * mine + 1 - parity) + half,
                        )

                    @pl.when(i >= DETOUR // PART)
                    def _():
                        send(
                            q_s.at[place],
                            q_r.at[place],
                            sem_s.at[8],
                            q_sem.at[n],
                            gate=2 * (2 * mine + below_parity) + half,
                            to_band=below,
                        )

                each(CHUNK // PART, part)

            @pl.when(band == bands - 1)
            def _():
                q_r[rows] = jnp.zeros((CHUNK, H), BF16)

        each(NCH, first_out)
        forward(1, m1, m1_sem)

        def second_one(n):
            @pl.when(band < bands - 1)
            def _():
                wait(q_r.at[0:CHUNK], q_sem.at[n])

            backward(1, q_r[chunk(n)].astype(F32), n, d3, ex_sem.at[1], sem_s.at[9])

        each(NCH, second_one)

        for i in range(3):
            wacc[:, i * H : (i + 1) * H] = dot_tn(m1[...], gbuf[:, i * H : (i + 1) * H])
        for i in range(4):
            eacc[:, i * H : (i + 1) * H] = dot_nn(xts[1], gbuf[:, i * H : (i + 1) * H])
        wait(d3.at[0:OWN], ex_sem.at[1])

        def second_zero(n):
            s = s0[chunk(n)] + collect(1, n, d3)
            backward(0, s, n, d4, ex_sem.at[2], sem_s.at[10])

        each(NCH, second_zero)
        for i in range(3):
            wacc[:, i * H : (i + 1) * H] += dot_tn(m0[...], gbuf[:, i * H : (i + 1) * H])
        for i in range(4):
            eacc[:, i * H : (i + 1) * H] += dot_nn(xts[0], gbuf[:, i * H : (i + 1) * H])
        halve(1, sem_s.at[11])

        wait(d4.at[0:OWN], ex_sem.at[2])

        @pl.when(band > 0)
        def _():
            wait(q_s, sem_s.at[8])

        def second_out(n):
            rows = chunk(n)
            q_s[rows] = collect(0, n, d4).astype(BF16)
            for e in range(2):
                k = 2 * n + e
                part = pl.ds(pl.multiple_of(k * ROWS, ROWS), ROWS)

                @pl.when(k == z)
                def _():
                    out[mine] = q_s[part]

                @pl.when(k != z)
                def _():
                    send(q_s.at[part], out.at[mine], sem_s.at[12], out_sem, gate=2 * k + half)

        each(NCH // 2, second_out)
        over_plane(1, plane_t.at[band // 2], sem_s.at[14])
        each(NCH // 2, lambda n: second_out(NCH // 2 + n))

    @pl.when(jnp.logical_not(active))
    def _():
        for _, buf, base, ssem, rsem in first_units:
            hand_on(buf, base, ssem, rsem)
        pl.semaphore_wait(plane_ready, rows_x - 1)
        over_plane(0, plane_r.at[band], sem_s.at[13])
        for i in range(1, 4):
            wait(m0.at[0 : 4 * ROWS + PASSED], sem_s.at[i])
        late()
        hand_on(*last_unit[1:])

        @pl.when(band > 0)
        def _():
            def pass_on(i):
                place = pl.ds(pl.multiple_of(i * PART, PART), PART)
                wait(q_r.at[0:PART], qp_sem.at[i])
                send(
                    q_r.at[place],
                    q_r.at[place],
                    sem_s.at[8],
                    q_sem.at[i // (CHUNK // PART)],
                    gate=2 * (2 * mine + below_parity) + half,
                    to_band=below,
                )

            pl.semaphore_wait(below_ready, 1)
            each(DETOUR // PART, pass_on)

    wait(plane_r.at[0 : bands - 1], wr_sem.at[1])

    @pl.when(active)
    def _():
        wait(plane_t.at[0 : bands // 2 - 1], wr_sem.at[3])

    @pl.when(jnp.logical_not(active))
    def _():
        wait(plane_t.at[0 : bands // 2], wr_sem.at[3])

    total = plane_r[0].astype(F32)
    for i in range(1, bands):
        total = total + plane_r[i].astype(F32)
    for i in range(bands // 2):
        total = total + plane_t[i].astype(F32)
    z_r[z] = total.astype(BF16)

    def along_z(i):
        peer = 2 * lax.rem(z + 1 + i, 8) + half
        send(z_r.at[z], z_r.at[z], sem_s.at[15], wr_sem.at[4], gate=peer)

    each(7, along_z)
    wait(z_r.at[0:7], wr_sem.at[4])
    total = z_r[0].astype(F32)
    for i in range(1, 8):
        total = total + z_r[i].astype(F32)
    total = total * (1.0 / math.sqrt(CIRC * bands * 2 * ROWS * GATES))
    done = piece_of(summed.at[half], band)
    done[...] = total.astype(BF16)

    def to_plane(i):
        peer = lax.rem(band + 1 + i, bands)
        send(done, done, sem_s.at[16], wr_sem.at[5], to_band=peer)

    each(bands - 1, to_plane)
    wait(plane_r.at[0 : bands - 1], wr_sem.at[5])
    send(summed.at[half], summed.at[half], sem_s.at[17], wr_sem.at[6], gate=sibling)
    wait(summed.at[half], wr_sem.at[6])

    @pl.when(active)
    def _():
        wait(out.at[0:3], out_sem)
        wait(idx_r.at[0, 0:3], sem_s.at[0])
        wait(idx_r.at[0], sem_s.at[18])
        wait(m0.at[0 : 3 * ROWS], sem_s.at[4])
        wait(d1.at[0:OWN], sem_s.at[6])
        wait(d1.at[0:OWN], sem_s.at[7])
        wait(d1.at[0:OWN], sem_s.at[9])
        wait(d1.at[0:OWN], sem_s.at[10])
        wait(half_r.at[1], sem_s.at[11])
        wait(q_s.at[0 : 7 * ROWS], sem_s.at[12])
        wait(plane_r.at[0 : bands - 1], sem_s.at[14])

    @pl.when(jnp.logical_not(active))
    def _():
        wait(out, out_sem)
        wait(idx_r.at[0, 0:4], sem_s.at[0])
        wait(m0.at[0 : 4 * ROWS + PASSED], sem_s.at[4])

        @pl.when(band > 0)
        def _():
            wait(q_r.at[0:DETOUR], sem_s.at[8])

    wait(half_r.at[0], sem_s.at[5])
    wait(plane_r.at[0 : bands - 1], sem_s.at[13])
    wait(z_r.at[0:7], sem_s.at[15])
    wait(plane_r.at[0 : bands - 1], sem_s.at[16])
    wait(summed.at[half], sem_s.at[17])


def finish_body(moved, summed, out, wout, bout, tout):
    out[...] = moved[...]
    for s in range(GATES):
        for n in range(3):
            wout[16 * s : 16 * s + 16, n * H : (n + 1) * H] = summed[s % 2, s // 2, n].astype(F32)
    for s in range(4):
        ext = summed[s % 2, s // 2, 3].astype(F32)
        if s != 2:
            n = min(s, 2)
            tout[:, n * H : (n + 1) * H] = ext[:8]
        if s < 3:
            bout[s * H : (s + 1) * H] = ext[8]


def shards(
    messages,
    gate_type,
    state_grad,
    fanin_owner,
    fanin_slot,
    live_count,
    hidden_weight,
    hidden_bias,
    type_table,
):
    bands = lax.axis_size("band")
    cols = min(8, bands)
    piece = (8 // cols, 4 // (bands // cols), 16, H)
    owners = jnp.swapaxes(fanin_owner[:, 0], 2, 3)
    slots = jnp.swapaxes(fanin_slot[:, 0], 2, 3)
    vmem = pl.BlockSpec(memory_space=pltpu.VMEM)
    dma = pltpu.SemaphoreType.DMA

    def body(*refs):
        kernel_body(bands, cols, *refs)

    moved, summed = pl.pallas_call(
        body,
        out_shape=(
            jax.ShapeDtypeStruct((CIRC, ROWS, H), BF16),
            jax.ShapeDtypeStruct((2,) + PIECES, BF16),
        ),
        in_specs=[vmem] * 5 + [pl.BlockSpec(memory_space=pltpu.SMEM)] + [vmem] * 3,
        out_specs=(vmem, vmem),
        scratch_shapes=[
            pltpu.VMEM((CIRC, 16, ROWS), jnp.int32),
            pltpu.VMEM((2, 8, 16, ROWS), jnp.int32),
            pltpu.VMEM((32, 3 * H), BF16),
            pltpu.VMEM((OWN, H), BF16),
            pltpu.VMEM((OWN, H), BF16),
            pltpu.VMEM((OWN, H), BF16),
            pltpu.VMEM((CIRC, ROWS, H), BF16),
            pltpu.VMEM((2 * OWN, H), BF16),
            pltpu.VMEM((2 * OWN, H), BF16),
            pltpu.VMEM((2 * OWN, H), BF16),
            pltpu.VMEM((2 * OWN, H), BF16),
            pltpu.VMEM((2, OWN, 2 * OWN), BF16),
            pltpu.VMEM((2, 5, OWN, H), F32),
            pltpu.VMEM((2, 16, OWN), BF16),
            pltpu.VMEM((OWN, H), F32),
            pltpu.VMEM((OWN, 4 * H), BF16),
            pltpu.VMEM((OWN, H), BF16),
            pltpu.VMEM((OWN, H), BF16),
            pltpu.VMEM((H, 3 * H), F32),
            pltpu.VMEM((16, 4 * H), F32),
            pltpu.VMEM((2, 2) + PIECES, BF16),
            pltpu.VMEM((2,) + PIECES, BF16),
            pltpu.VMEM((2,) + PIECES, BF16),
            pltpu.VMEM((bands,) + piece, BF16),
            pltpu.VMEM((max(bands // 2, 1),) + piece, BF16),
            pltpu.VMEM((8,) + piece, BF16),
            dma((19,)),
            dma,
            dma,
            dma((8,)),
            dma((8,)),
            dma((8,)),
            dma((8,)),
            dma,
            dma((3,)),
            dma((NCH,)),
            dma((DETOUR // PART,)),
            dma,
            dma((7,)),
            pltpu.SemaphoreType.REGULAR,
            pltpu.SemaphoreType.REGULAR,
            pltpu.SemaphoreType.REGULAR,
        ],
        compiler_params=pltpu.CompilerParams(
            collective_id=0, has_side_effects=True, vmem_limit_bytes=56 * 1024 * 1024
        ),
        name="band_passes",
    )(
        messages[:, 0],
        gate_type[:, 0],
        state_grad[:, 0],
        owners,
        slots,
        live_count[:, 0].T,
        hidden_weight,
        hidden_bias,
        type_table,
    )
    out, weight, bias, rows = pl.pallas_call(
        finish_body,
        out_shape=(
            jax.ShapeDtypeStruct((CIRC, ROWS, H), BF16),
            jax.ShapeDtypeStruct((H, 3 * H), F32),
            jax.ShapeDtypeStruct((3 * H,), F32),
            jax.ShapeDtypeStruct((8, 3 * H), F32),
        ),
        in_specs=[vmem] * 2,
        out_specs=(vmem,) * 4,
        name="results",
    )(moved, summed)
    return out[:, None], weight, bias, rows


def solution(mesh):
    return jax.shard_map(
        shards,
        mesh=mesh,
        in_specs=(
            P(None, "band", None, "gate", None),
            P(None, "band", None, "gate"),
            P(None, "band", None, "gate", None),
            P(None, "band", None, "gate", None),
            P(None, "band", None, "gate", None),
            P(None, "band", None),
            P(),
            P(),
            P(),
        ),
        out_specs=(P(None, "band", "gate", None), P(), P(), P()),
        check_vma=False,
    )
```

```python
import math

import jax
import jax.numpy as jnp
from jax import lax
from jax.experimental import pallas as pl
from jax.experimental.pallas import tpu as pltpu
from jax.sharding import PartitionSpec as P

F32 = jnp.float32
BF16 = jnp.bfloat16
H = 256
ROWS = 128
GATES = 16
CIRC = 4
OWN = 1024
CHUNK = 256
NCH = OWN // CHUNK
PART = 64
PASSED = 5 * ROWS // 2
DETOUR = 384
PIECES = (4, 8, 16, H)


def iota(shape, dim):
    return lax.broadcasted_iota(jnp.int32, shape, dim)


def dot_tn(a, b):
    return lax.dot_general(a, b, (((0,), (0,)), ((), ())), preferred_element_type=F32)


def dot_nt(a, b):
    return lax.dot_general(a, b, (((1,), (1,)), ((), ())), preferred_element_type=F32)


def dot_nn(a, b):
    return jnp.dot(a, b, preferred_element_type=F32)


def kernel_body(
    bands,
    cols,
    msg,
    types,
    sg,
    owner,
    slot,
    live,
    w,
    bias,
    table,
    out,
    summed,
    idx_s,
    idx_r,
    pieces,
    m0,
    sg0,
    m1,
    dm_s,
    d1,
    d2,
    d3,
    d4,
    sel,
    coef,
    xts,
    s0,
    gbuf,
    q_s,
    q_r,
    wacc,
    eacc,
    msg1,
    sg1,
    half_s,
    half_r,
    plane_s,
    plane_r,
    z_r,
    sem_s,
    idx_sem,
    fi_sem,
    m0_sem,
    sg0_sem,
    dm_sem,
    m1_sem,
    fw_sem,
    ex_sem,
    q_sem,
    qp_sem,
    out_sem,
    wr_sem,
    ax_sem,
    own_sem,
    pair_ready,
    below_ready,
    plane_ready,
):
    rows_y = cols
    rows_x = bands // cols
    me = lax.axis_index("gate")
    band = lax.axis_index("band")
    z = me // 2
    half = lax.rem(me, 2)
    mine = z // 2
    sibling = me + 1 - 2 * half
    by = lax.rem(band, rows_y)
    bx = band // rows_y

    def parity_of(b):
        return lax.rem(b + b // rows_y, 2)

    parity = parity_of(band)
    active = lax.rem(z, 2) == parity
    below = jnp.maximum(band - 1, 0)
    below_parity = parity_of(below)
    beside_y = bx * rows_y + by + 1 - 2 * lax.rem(by, 2)
    beside_x = (bx + 1 - 2 * lax.rem(bx, 2)) * rows_y + by if rows_x > 1 else beside_y

    def send(src, dst, ssem, rsem, gate=None, to_band=None):
        where = {}
        if to_band is not None:
            where["band"] = to_band
        if gate is not None:
            where["gate"] = gate
        pltpu.make_async_remote_copy(
            src_ref=src,
            dst_ref=dst,
            send_sem=ssem,
            recv_sem=rsem,
            device_id=where,
            device_id_type=pl.DeviceIdType.MESH,
        ).start()

    def wait(ref, sem):
        pltpu.make_async_copy(ref, ref, sem).wait()

    def each(count, body):
        def step(i, carry):
            body(i)
            return carry

        lax.fori_loop(0, count, step, 0)

    load_m = pltpu.make_async_copy(msg.at[:, 1], msg1, own_sem.at[0])
    load_s = pltpu.make_async_copy(sg.at[:, 1], sg1, own_sem.at[1])
    load_m.start()
    load_s.start()

    barrier = pltpu.get_barrier_semaphore()

    def greet(**where):
        pl.semaphore_signal(
            barrier, inc=1, device_id=where, device_id_type=pl.DeviceIdType.MESH
        )

    each(7, lambda i: greet(gate=lax.rem(me + 2 + 2 * i, GATES)))
    greet(gate=sibling)
    each(rows_y - 1, lambda i: greet(band=bx * rows_y + lax.rem(by + 1 + i, rows_y)))
    if rows_x > 1:
        each(rows_x - 1, lambda i: greet(band=lax.rem(bx + 1 + i, rows_x) * rows_y + by))
    greet(band=lax.rem(band + 1, bands))
    greet(band=lax.rem(band + bands - 1, bands))

    for c in range(CIRC):
        for lv in range(2):
            idx_s[c, 4 * lv : 4 * lv + 4, :] = owner[c, lv] * ROWS + slot[c, lv]
        idx_s[c, 8:10, :] = types[c]
        idx_s[c, 10:16, :] = jnp.zeros((6, ROWS), jnp.int32)
    full_bias = bias[...].reshape(1, 3 * H)
    full = table[...] + jnp.where(iota((8, 3 * H), 1) < 2 * H, full_bias, 0.0)
    hi = full.astype(BF16)
    rest = full - hi.astype(F32)
    mid = rest.astype(BF16)
    low = (rest - mid.astype(F32)).astype(BF16)
    pieces[...] = jnp.concatenate(
        [hi.astype(F32), mid.astype(F32), low.astype(F32), jnp.zeros((8, 3 * H), F32)], axis=0
    ).astype(BF16)
    cand_bias = full_bias[:, 2 * H :]

    def coefficients(m, kinds, gate0, count):
        hot = jnp.where(lax.bitwise_and(iota((32, ROWS), 0), 7) == kinds, 1.0, 0.0).astype(BF16)
        inp = dot_tn(hot, pieces[...])
        pre = dot_nn(m, w[...])
        tr = jnp.tanh(0.5 * (inp[:, :H] + pre[:, :H]))
        tu = jnp.tanh(0.5 * (inp[:, H : 2 * H] + pre[:, H : 2 * H]))
        cand = pre[:, 2 * H :] + cand_bias
        r = 0.5 + 0.5 * tr
        u = 0.5 + 0.5 * tu
        new = jnp.tanh(inp[:, 2 * H :] + r * cand)
        on = jnp.where(iota((ROWS, 1), 0) + gate0 < count, 1.0, 0.0)
        a = (1.0 - u) * (1.0 - new * new) * on
        dc = a * r
        dr = a * cand * (r * (1.0 - r))
        dz = (m.astype(F32) - new) * (u * (1.0 - u)) * on
        return a, dr, dz, dc, u * on

    def kinds_ext(kinds):
        row = iota((16, ROWS), 0)
        return jnp.where(jnp.logical_or(row == kinds, row == 8), 1.0, 0.0).astype(BF16)

    def grads(s, factors):
        a, b, c, d, u = factors
        dr = (s * b).astype(BF16)
        dz = (s * c).astype(BF16)
        dc = (s * d).astype(BF16)
        dn = (s * a).astype(BF16)
        down = (
            s * u
            + dot_nt(dr, w[:, :H])
            + dot_nt(dz, w[:, H : 2 * H])
            + dot_nt(dc, w[:, 2 * H :])
        )
        return dr, dz, dc, dn, down.astype(BF16)

    wacc[...] = jnp.zeros_like(wacc)
    eacc[...] = jnp.zeros_like(eacc)

    def level_one(c):
        m = msg1[c]
        kinds = types[c, 1:2, :]
        factors = coefficients(m, kinds, me * ROWS, live[1, c])
        dr, dz, dc, dn, down = grads(sg1[c].astype(F32), factors)
        dm_s[c] = down
        ext = kinds_ext(kinds)
        for i, g in enumerate((dr, dz, dc)):
            wacc[:, i * H : (i + 1) * H] += dot_tn(m, g)
        for i, g in enumerate((dr, dz, dc, dn)):
            eacc[:, i * H : (i + 1) * H] += dot_nn(ext, g)

    load_m.wait()
    load_s.wait()
    each(CIRC, level_one)

    pl.semaphore_wait(barrier, 8 + rows_y - 1 + rows_x - 1 + 2)
    each(
        rows_x - 1,
        lambda i: pl.semaphore_signal(
            plane_ready,
            inc=1,
            device_id={"band": lax.rem(bx + 1 + i, rows_x) * rows_y + by},
            device_id_type=pl.DeviceIdType.MESH,
        ),
    )
    for b in (beside_y, beside_x)[: min(rows_x, 2)]:
        pl.semaphore_signal(
            pair_ready, inc=1, device_id={"band": b}, device_id_type=pl.DeviceIdType.MESH
        )

    @pl.when(band < bands - 1)
    def _():
        pl.semaphore_signal(
            below_ready,
            inc=1,
            device_id={"band": jnp.minimum(band + 1, bands - 1)},
            device_id_type=pl.DeviceIdType.MESH,
        )

    def block(k):
        return pl.ds(pl.multiple_of(k * ROWS, ROWS), ROWS)

    def half_block(k, e):
        return pl.ds(pl.multiple_of(k * ROWS + e * (ROWS // 2), ROWS // 2), ROWS // 2)

    def steps_to(c):
        return lax.rem(2 * c + parity + 8 - z, 8)

    def gate_of(c):
        return 2 * (2 * c + parity) + half

    top, bottom = pl.ds(0, ROWS // 2), pl.ds(ROWS // 2, ROWS // 2)

    def to_task(src_of, buf, base, ssem, rsem):
        for c in range(CIRC):
            steps = steps_to(c)

            @pl.when(steps == 0)
            def _():
                pltpu.make_async_copy(src_of(c), buf.at[block(base + z)], rsem.at[z]).start()

            @pl.when(steps == 4)
            def _():
                send(
                    src_of(c).at[top],
                    buf.at[half_block(base + z, 0)],
                    ssem,
                    rsem.at[z],
                    gate=gate_of(c),
                )

            @pl.when(
                jnp.logical_and(
                    jnp.logical_and(steps != 0, steps != 4),
                    jnp.logical_and(steps != 1, steps != 7),
                )
            )
            def _():
                send(src_of(c), buf.at[block(base + z)], ssem, rsem.at[z], gate=gate_of(c))

    def to_task_by(src_of, buf, base, ssem, rsem):
        for c in range(CIRC):
            steps = steps_to(c)

            @pl.when(steps == 1)
            def _():
                send(
                    src_of(c),
                    buf.at[block(base + z)],
                    ssem,
                    rsem.at[z],
                    gate=gate_of(c),
                    to_band=beside_y,
                )

            @pl.when(steps == 4)
            def _():
                send(
                    src_of(c).at[bottom],
                    buf.at[half_block(base + z, 1)],
                    ssem,
                    rsem.at[z],
                    gate=gate_of(c),
                    to_band=beside_y,
                )

            @pl.when(steps == 7)
            def _():
                send(
                    src_of(c),
                    buf.at[block(base + z)],
                    ssem,
                    rsem.at[z],
                    gate=gate_of(c),
                    to_band=beside_x,
                )

    def hand_on(buf, base, ssem, rsem):
        for steps, b in ((1, beside_y), (7, beside_x), (4, beside_y)):
            k = lax.rem(z + 8 - steps, 8)
            place = half_block(base + k, 1) if steps == 4 else block(base + k)
            wait(buf.at[0 : ROWS // 2] if steps == 4 else buf.at[0:ROWS], rsem.at[k])
            send(buf.at[place], buf.at[place], ssem, rsem.at[k], to_band=b)

    for c in range(CIRC):

        @pl.when(steps_to(c) == 0)
        def _():
            idx_r[half, z] = idx_s[c]

        @pl.when(steps_to(c) != 0)
        def _():
            send(idx_s.at[c], idx_r.at[half, z], sem_s.at[0], idx_sem, gate=gate_of(c))

    first_units = (
        (lambda c: dm_s.at[c], d1, 8 * half, sem_s.at[3], dm_sem),
        (lambda c: msg.at[c, 0], m0, 0, sem_s.at[1], m0_sem),
        (lambda c: sg.at[c, 0], sg0, 0, sem_s.at[2], sg0_sem),
    )
    last_unit = (lambda c: msg1.at[c], m1, 0, sem_s.at[4], m1_sem)
    to_task(*first_units[0])
    pl.semaphore_wait(pair_ready, min(rows_x, 2))
    to_task_by(*first_units[0])
    for unit in first_units[1:]:
        to_task_by(*unit)
        to_task(*unit)
    py, px = 8 // rows_y, 4 // rows_x

    def x_part(ref, x):
        return ref.at[pl.ds(x * px, px)]

    def piece_of(ref, to):
        return ref.at[pl.ds((to // rows_y) * px, px), pl.ds(lax.rem(to, rows_y) * py, py)]

    def halve():
        for i in range(GATES):
            for n in range(3):
                half_s[i % 2, n, i // 2] = wacc[16 * i : 16 * i + 16, n * H : (n + 1) * H].astype(
                    BF16
                )
            if i < 4:
                half_s[i % 2, 3, i // 2] = eacc[:, i * H : (i + 1) * H].astype(BF16)
            else:
                half_s[i % 2, 3, i // 2] = jnp.zeros((16, H), BF16)
        send(half_s.at[1 - half], half_r, sem_s.at[5], wr_sem.at[0], gate=sibling)

    def over_plane():
        wait(half_r, wr_sem.at[0])
        for n in range(4):
            plane_s[n] = (half_s[half, n].astype(F32) + half_r[n].astype(F32)).astype(BF16)
        pl.semaphore_wait(plane_ready, rows_x - 1)

        def to(i):
            peer = lax.rem(band + 1 + i, bands)
            send(piece_of(plane_s, peer), plane_r.at[band], sem_s.at[11], wr_sem.at[1], to_band=peer)

        each(bands - 1, to)
        plane_r[band] = piece_of(plane_s, band)[...]

    def along_ring():
        wait(plane_r.at[0 : bands - 1], wr_sem.at[1])
        total = plane_r[0].astype(F32)
        for i in range(1, bands):
            total = total + plane_r[i].astype(F32)
        z_r[z] = total.astype(BF16)

        def to(i):
            peer = 2 * lax.rem(z + 1 + i, 8) + half
            send(z_r.at[z], z_r.at[z], sem_s.at[15], wr_sem.at[4], gate=peer)

        each(7, to)

    def late():
        to_task(*last_unit)
        to_task_by(*last_unit)

    def turn(t):
        off = jnp.where(lax.rem(t, 2) == 1, (t + 1) // 2, 8 - t // 2)
        return lax.rem(z + off, 8)

    @pl.when(active)
    def _():
        wait(idx_r.at[0, 0:7], idx_sem)
        send(idx_r.at[half], idx_r.at[half], sem_s.at[18], fi_sem, gate=sibling)

        def build(j):
            tile = idx_r[j // 8, lax.rem(j, 8)]
            col = pl.ds(pl.multiple_of(j * ROWS, ROWS), ROWS)
            spot = iota((ROWS, ROWS), 0)
            block = 2 * iota((8, ROWS), 0) + half
            for lv in (1, 0):
                at = jnp.full((8, ROWS), -1, jnp.int32)
                for f in range(4):
                    t = tile[4 * lv + f : 4 * lv + f + 1, :]
                    at = jnp.where(
                        lax.shift_right_logical(t, 7) == block, lax.bitwise_and(t, 127), at
                    )
                for k in range(8):
                    sel[lv, k * ROWS : (k + 1) * ROWS, col] = jnp.where(
                        spot == at[k : k + 1, :], 1.0, 0.0
                    ).astype(BF16)

        each(8, lambda k: build(8 * half + k))
        wait(idx_r.at[0], fi_sem)
        each(8, lambda k: build(8 - 8 * half + k))

        def forward(lv, m_ref, sem):
            def step(t):
                k = turn(t)

                wait(m_ref.at[0:ROWS], sem.at[k])
                rows = pl.ds(pl.multiple_of(k * ROWS, ROWS), ROWS)
                j = 2 * k + half
                kinds = idx_r[half, k, 8 + lv : 9 + lv, :]
                factors = coefficients(m_ref[rows], kinds, j * ROWS, live[lv, mine])
                for i, f in enumerate(factors):
                    coef[lv, i, rows] = f
                xts[lv, :, rows] = kinds_ext(kinds)

            each(8, step)

        forward(0, m0, m0_sem)
        for i in range(1, 4):
            wait(m0.at[0 : 3 * ROWS], sem_s.at[i])
        late()

        def relay(t):
            k = turn(t)
            rows = pl.ds(pl.multiple_of(half * OWN + k * ROWS, ROWS), ROWS)

            wait(d1.at[0:ROWS], dm_sem.at[k])
            send(d1.at[rows], d1.at[rows], sem_s.at[6], fw_sem, gate=sibling)

        each(8, relay)
        each(8, lambda i: wait(sg0.at[0:ROWS], sg0_sem.at[i]))
        wait(d1.at[0:OWN], fw_sem)

        def chunk(n):
            return pl.ds(pl.multiple_of(n * CHUNK, CHUNK), CHUNK)

        def backward(lv, s, n, dst, sem, ssem):
            rows = chunk(n)
            factors = tuple(coef[lv, i, rows] for i in range(5))
            dr, dz, dc, dn, down = grads(s, factors)
            for i, g in enumerate((dr, dz, dc, dn)):
                gbuf[rows, i * H : (i + 1) * H] = g
            place = pl.ds(pl.multiple_of(half * OWN + n * CHUNK, CHUNK), CHUNK)
            dst[place] = down
            send(dst.at[place], dst.at[place], ssem, sem, gate=sibling)

        def collect(lv, n, src):
            return dot_nn(sel[lv, chunk(n)], src[...])

        @pl.when(band > 0)
        def _():
            pl.semaphore_wait(below_ready, 1)

        def first_zero(n):
            s = sg0[chunk(n)].astype(F32) + collect(1, n, d1)
            s0[chunk(n)] = s
            backward(0, s, n, d2, ex_sem.at[0], sem_s.at[7])

        each(NCH, first_zero)
        wait(d2.at[0:OWN], ex_sem.at[0])

        def first_out(n):
            rows = chunk(n)
            q_s[rows] = collect(0, n, d2).astype(BF16)

            @pl.when(band > 0)
            def _():
                def part(e):
                    i = n * (CHUNK // PART) + e
                    place = pl.ds(pl.multiple_of(i * PART, PART), PART)

                    @pl.when(i < DETOUR // PART)
                    def _():
                        send(
                            q_s.at[place],
                            q_r.at[place],
                            sem_s.at[8],
                            qp_sem.at[i],
                            gate=2 * (2 * mine + 1 - parity) + half,
                        )

                    @pl.when(i >= DETOUR // PART)
                    def _():
                        send(
                            q_s.at[place],
                            q_r.at[place],
                            sem_s.at[8],
                            q_sem.at[n],
                            gate=2 * (2 * mine + below_parity) + half,
                            to_band=below,
                        )

                each(CHUNK // PART, part)

            @pl.when(band == bands - 1)
            def _():
                q_r[rows] = jnp.zeros((CHUNK, H), BF16)

        each(NCH, first_out)
        forward(1, m1, m1_sem)

        def second_one(n):
            @pl.when(band < bands - 1)
            def _():
                wait(q_r.at[0:CHUNK], q_sem.at[n])

            backward(1, q_r[chunk(n)].astype(F32), n, d3, ex_sem.at[1], sem_s.at[9])

        each(NCH, second_one)

        for i in range(3):
            wacc[:, i * H : (i + 1) * H] += dot_tn(m1[...], gbuf[:, i * H : (i + 1) * H])
        for i in range(4):
            eacc[:, i * H : (i + 1) * H] += dot_nn(xts[1], gbuf[:, i * H : (i + 1) * H])
        wait(d3.at[0:OWN], ex_sem.at[1])

        def second_zero(n):
            s = s0[chunk(n)] + collect(1, n, d3)
            backward(0, s, n, d4, ex_sem.at[2], sem_s.at[10])

        each(NCH, second_zero)
        for i in range(3):
            wacc[:, i * H : (i + 1) * H] += dot_tn(m0[...], gbuf[:, i * H : (i + 1) * H])
        for i in range(4):
            eacc[:, i * H : (i + 1) * H] += dot_nn(xts[0], gbuf[:, i * H : (i + 1) * H])
        halve()

        wait(d4.at[0:OWN], ex_sem.at[2])

        @pl.when(band > 0)
        def _():
            wait(q_s, sem_s.at[8])

        def second_out(n):
            q_s[chunk(n)] = collect(0, n, d4).astype(BF16)

        def deliver(k):
            @pl.when(k == z)
            def _():
                out[mine] = q_s[block(k)]

            @pl.when(k != z)
            def _():
                send(q_s.at[block(k)], out.at[mine], sem_s.at[12], out_sem, gate=2 * k + half)

        def second_out_now(n):
            second_out(n)
            deliver(2 * n)
            deliver(2 * n + 1)

        each(NCH // 2, second_out_now)
        over_plane()
        each(NCH // 2, lambda n: second_out(NCH // 2 + n))
        along_ring()
        each(4, lambda k: deliver(4 + k))

    @pl.when(jnp.logical_not(active))
    def _():
        for _, buf, base, ssem, rsem in first_units:
            hand_on(buf, base, ssem, rsem)
        for i in range(1, 4):
            wait(m0.at[0 : 4 * ROWS + PASSED], sem_s.at[i])
        late()
        hand_on(*last_unit[1:])

        @pl.when(band > 0)
        def _():
            def pass_on(i):
                place = pl.ds(pl.multiple_of(i * PART, PART), PART)
                wait(q_r.at[0:PART], qp_sem.at[i])
                send(
                    q_r.at[place],
                    q_r.at[place],
                    sem_s.at[8],
                    q_sem.at[i // (CHUNK // PART)],
                    gate=2 * (2 * mine + below_parity) + half,
                    to_band=below,
                )

            pl.semaphore_wait(below_ready, 1)
            each(DETOUR // PART, pass_on)

        halve()
        over_plane()
        along_ring()

    wait(z_r.at[0:7], wr_sem.at[4])
    total = z_r[0].astype(F32)
    for i in range(1, 8):
        total = total + z_r[i].astype(F32)
    total = total * (1.0 / math.sqrt(CIRC * bands * 2 * ROWS * GATES))
    done = piece_of(summed.at[half], band)
    done[...] = total.astype(BF16)

    def to_plane(i):
        peer = lax.rem(band + 1 + i, bands)
        send(done, done, sem_s.at[16], ax_sem.at[bx], to_band=peer)

    each(bands - 1, to_plane)

    def to_sibling(i):
        x = lax.rem(bx + i, rows_x)
        there = x_part(summed.at[half], x)

        @pl.when(i == 0)
        def _():
            wait(plane_r.at[0 : rows_y - 1], ax_sem.at[x])

        @pl.when(i > 0)
        def _():
            wait(plane_r.at[0:rows_y], ax_sem.at[x])

        send(there, there, sem_s.at[17], wr_sem.at[6], gate=sibling)

    each(rows_x, to_sibling)
    wait(summed.at[half], wr_sem.at[6])

    @pl.when(active)
    def _():
        wait(out.at[0:3], out_sem)
        wait(idx_r.at[0, 0:3], sem_s.at[0])
        wait(idx_r.at[0], sem_s.at[18])
        wait(m0.at[0 : 3 * ROWS], sem_s.at[4])
        wait(d1.at[0:OWN], sem_s.at[6])
        wait(d1.at[0:OWN], sem_s.at[7])
        wait(d1.at[0:OWN], sem_s.at[9])
        wait(d1.at[0:OWN], sem_s.at[10])
        wait(q_s.at[0 : 7 * ROWS], sem_s.at[12])

    @pl.when(jnp.logical_not(active))
    def _():
        wait(out, out_sem)
        wait(idx_r.at[0, 0:4], sem_s.at[0])
        wait(m0.at[0 : 4 * ROWS + PASSED], sem_s.at[4])

        @pl.when(band > 0)
        def _():
            wait(q_r.at[0:DETOUR], sem_s.at[8])

    wait(half_r, sem_s.at[5])
    wait(plane_r.at[0 : bands - 1], sem_s.at[11])
    wait(z_r.at[0:7], sem_s.at[15])
    wait(plane_r.at[0 : bands - 1], sem_s.at[16])
    wait(summed.at[half], sem_s.at[17])


def finish_body(moved, summed, out, wout, bout, tout):
    out[...] = moved[...]
    for s in range(GATES):
        for n in range(3):
            wout[16 * s : 16 * s + 16, n * H : (n + 1) * H] = summed[s % 2, n, s // 2].astype(F32)
    for s in range(4):
        ext = summed[s % 2, 3, s // 2].astype(F32)
        if s != 2:
            n = min(s, 2)
            tout[:, n * H : (n + 1) * H] = ext[:8]
        if s < 3:
            bout[s * H : (s + 1) * H] = ext[8]


def shards(
    messages,
    gate_type,
    state_grad,
    fanin_owner,
    fanin_slot,
    live_count,
    hidden_weight,
    hidden_bias,
    type_table,
):
    bands = lax.axis_size("band")
    cols = min(8, bands)
    rows_x = bands // cols
    py, px = 8 // cols, 4 // rows_x
    owners = jnp.swapaxes(fanin_owner[:, 0], 2, 3)
    slots = jnp.swapaxes(fanin_slot[:, 0], 2, 3)
    vmem = pl.BlockSpec(memory_space=pltpu.VMEM)
    hbm = pl.BlockSpec(memory_space=pl.ANY)
    dma = pltpu.SemaphoreType.DMA

    def body(*refs):
        kernel_body(bands, cols, *refs)

    moved, summed = pl.pallas_call(
        body,
        out_shape=(
            jax.ShapeDtypeStruct((CIRC, ROWS, H), BF16),
            jax.ShapeDtypeStruct((2,) + PIECES, BF16),
        ),
        in_specs=[hbm, vmem, hbm, vmem, vmem, pl.BlockSpec(memory_space=pltpu.SMEM)] + [vmem] * 3,
        out_specs=(vmem, vmem),
        scratch_shapes=[
            pltpu.VMEM((CIRC, 16, ROWS), jnp.int32),
            pltpu.VMEM((2, 8, 16, ROWS), jnp.int32),
            pltpu.VMEM((32, 3 * H), BF16),
            pltpu.VMEM((OWN, H), BF16),
            pltpu.VMEM((OWN, H), BF16),
            pltpu.VMEM((OWN, H), BF16),
            pltpu.VMEM((CIRC, ROWS, H), BF16),
            pltpu.VMEM((2 * OWN, H), BF16),
            pltpu.VMEM((2 * OWN, H), BF16),
            pltpu.VMEM((2 * OWN, H), BF16),
            pltpu.VMEM((2 * OWN, H), BF16),
            pltpu.VMEM((2, OWN, 2 * OWN), BF16),
            pltpu.VMEM((2, 5, OWN, H), F32),
            pltpu.VMEM((2, 16, OWN), BF16),
            pltpu.VMEM((OWN, H), F32),
            pltpu.VMEM((OWN, 4 * H), BF16),
            pltpu.VMEM((OWN, H), BF16),
            pltpu.VMEM((OWN, H), BF16),
            pltpu.VMEM((H, 3 * H), F32),
            pltpu.VMEM((16, 4 * H), F32),
            pltpu.VMEM((CIRC, ROWS, H), BF16),
            pltpu.VMEM((CIRC, ROWS, H), BF16),
            pltpu.VMEM((2,) + PIECES, BF16),
            pltpu.VMEM(PIECES, BF16),
            pltpu.VMEM(PIECES, BF16),
            pltpu.VMEM((bands, px, py, 16, H), BF16),
            pltpu.VMEM((8, px, py, 16, H), BF16),
            dma((19,)),
            dma,
            dma,
            dma((8,)),
            dma((8,)),
            dma((8,)),
            dma((8,)),
            dma,
            dma((3,)),
            dma((NCH,)),
            dma((DETOUR // PART,)),
            dma,
            dma((7,)),
            dma((rows_x,)),
            dma((2,)),
            pltpu.SemaphoreType.REGULAR,
            pltpu.SemaphoreType.REGULAR,
            pltpu.SemaphoreType.REGULAR,
        ],
        compiler_params=pltpu.CompilerParams(
            collective_id=0, has_side_effects=True, vmem_limit_bytes=56 * 1024 * 1024
        ),
        name="band_passes",
    )(
        messages[:, 0],
        gate_type[:, 0],
        state_grad[:, 0],
        owners,
        slots,
        live_count[:, 0].T,
        hidden_weight,
        hidden_bias,
        type_table,
    )
    out, weight, bias, rows = pl.pallas_call(
        finish_body,
        out_shape=(
            jax.ShapeDtypeStruct((CIRC, ROWS, H), BF16),
            jax.ShapeDtypeStruct((H, 3 * H), F32),
            jax.ShapeDtypeStruct((3 * H,), F32),
            jax.ShapeDtypeStruct((8, 3 * H), F32),
        ),
        in_specs=[vmem] * 2,
        out_specs=(vmem,) * 4,
        name="results",
    )(moved, summed)
    return out[:, None], weight, bias, rows


def solution(mesh):
    return jax.shard_map(
        shards,
        mesh=mesh,
        in_specs=(
            P(None, "band", None, "gate", None),
            P(None, "band", None, "gate"),
            P(None, "band", None, "gate", None),
            P(None, "band", None, "gate", None),
            P(None, "band", None, "gate", None),
            P(None, "band", None),
            P(),
            P(),
            P(),
        ),
        out_specs=(P(None, "band", "gate", None), P(), P(), P()),
        check_vma=False,
    )
```

```python
import math

import jax
import jax.numpy as jnp
from jax import lax
from jax.experimental import pallas as pl
from jax.experimental.pallas import tpu as pltpu
from jax.sharding import PartitionSpec as P

F32 = jnp.float32
BF16 = jnp.bfloat16
H = 256
ROWS = 128
GATES = 16
CIRC = 4
OWN = 1024
CHUNK = 256
NCH = OWN // CHUNK
PART = 64
PASSED = 5 * ROWS // 2
DETOUR = 384
PIECES = (4, 8, 16, H)


def iota(shape, dim):
    return lax.broadcasted_iota(jnp.int32, shape, dim)


def dot_tn(a, b):
    return lax.dot_general(a, b, (((0,), (0,)), ((), ())), preferred_element_type=F32)


def dot_nt(a, b):
    return lax.dot_general(a, b, (((1,), (1,)), ((), ())), preferred_element_type=F32)


def dot_nn(a, b):
    return jnp.dot(a, b, preferred_element_type=F32)


def kernel_body(
    bands,
    cols,
    msg,
    types,
    sg,
    owner,
    slot,
    live,
    w,
    bias,
    table,
    out,
    summed,
    idx_s,
    idx_r,
    pieces,
    m0,
    sg0,
    m1,
    dm_s,
    d1,
    d2,
    d3,
    d4,
    sel,
    coef,
    xts,
    s0,
    gbuf,
    q_s,
    q_r,
    wacc,
    eacc,
    msg1,
    sg1,
    half_s,
    half_r,
    plane_s,
    plane_r,
    z_r,
    sem_s,
    idx_sem,
    fi_sem,
    m0_sem,
    sg0_sem,
    dm_sem,
    m1_sem,
    fw_sem,
    ex_sem,
    q_sem,
    qp_sem,
    out_sem,
    wr_sem,
    ax_sem,
    own_sem,
    pair_ready,
    below_ready,
    plane_ready,
):
    rows_y = cols
    rows_x = bands // cols
    me = lax.axis_index("gate")
    band = lax.axis_index("band")
    z = me // 2
    half = lax.rem(me, 2)
    mine = z // 2
    sibling = me + 1 - 2 * half
    by = lax.rem(band, rows_y)
    bx = band // rows_y

    def parity_of(b):
        return lax.rem(b + b // rows_y, 2)

    parity = parity_of(band)
    active = lax.rem(z, 2) == parity
    below = jnp.maximum(band - 1, 0)
    below_parity = parity_of(below)
    beside_y = bx * rows_y + by + 1 - 2 * lax.rem(by, 2)
    beside_x = (bx + 1 - 2 * lax.rem(bx, 2)) * rows_y + by if rows_x > 1 else beside_y

    def send(src, dst, ssem, rsem, gate=None, to_band=None):
        where = {}
        if to_band is not None:
            where["band"] = to_band
        if gate is not None:
            where["gate"] = gate
        pltpu.make_async_remote_copy(
            src_ref=src,
            dst_ref=dst,
            send_sem=ssem,
            recv_sem=rsem,
            device_id=where,
            device_id_type=pl.DeviceIdType.MESH,
        ).start()

    def wait(ref, sem):
        pltpu.make_async_copy(ref, ref, sem).wait()

    def each(count, body):
        def step(i, carry):
            body(i)
            return carry

        lax.fori_loop(0, count, step, 0)

    load_m = pltpu.make_async_copy(msg.at[:, 1], msg1, own_sem.at[0])
    load_s = pltpu.make_async_copy(sg.at[:, 1], sg1, own_sem.at[1])
    load_m.start()
    load_s.start()

    barrier = pltpu.get_barrier_semaphore()

    def greet(**where):
        pl.semaphore_signal(
            barrier, inc=1, device_id=where, device_id_type=pl.DeviceIdType.MESH
        )

    each(7, lambda i: greet(gate=lax.rem(me + 2 + 2 * i, GATES)))
    greet(gate=sibling)
    each(rows_y - 1, lambda i: greet(band=bx * rows_y + lax.rem(by + 1 + i, rows_y)))
    if rows_x > 1:
        each(rows_x - 1, lambda i: greet(band=lax.rem(bx + 1 + i, rows_x) * rows_y + by))
    greet(band=lax.rem(band + 1, bands))
    greet(band=lax.rem(band + bands - 1, bands))

    for c in range(CIRC):
        for lv in range(2):
            idx_s[c, 4 * lv : 4 * lv + 4, :] = owner[c, lv] * ROWS + slot[c, lv]
        idx_s[c, 8:10, :] = types[c]
        idx_s[c, 10:16, :] = jnp.zeros((6, ROWS), jnp.int32)
    full_bias = bias[...].reshape(1, 3 * H)
    full = table[...] + jnp.where(iota((8, 3 * H), 1) < 2 * H, full_bias, 0.0)
    hi = full.astype(BF16)
    rest = full - hi.astype(F32)
    mid = rest.astype(BF16)
    low = (rest - mid.astype(F32)).astype(BF16)
    pieces[...] = jnp.concatenate(
        [hi.astype(F32), mid.astype(F32), low.astype(F32), jnp.zeros((8, 3 * H), F32)], axis=0
    ).astype(BF16)
    cand_bias = full_bias[:, 2 * H :]

    def coefficients(m, kinds, gate0, count):
        hot = jnp.where(lax.bitwise_and(iota((32, ROWS), 0), 7) == kinds, 1.0, 0.0).astype(BF16)
        inp = dot_tn(hot, pieces[...])
        pre = dot_nn(m, w[...])
        tr = jnp.tanh(0.5 * (inp[:, :H] + pre[:, :H]))
        tu = jnp.tanh(0.5 * (inp[:, H : 2 * H] + pre[:, H : 2 * H]))
        cand = pre[:, 2 * H :] + cand_bias
        r = 0.5 + 0.5 * tr
        u = 0.5 + 0.5 * tu
        new = jnp.tanh(inp[:, 2 * H :] + r * cand)
        on = jnp.where(iota((ROWS, 1), 0) + gate0 < count, 1.0, 0.0)
        a = (1.0 - u) * (1.0 - new * new) * on
        dc = a * r
        dr = a * cand * (r * (1.0 - r))
        dz = (m.astype(F32) - new) * (u * (1.0 - u)) * on
        return a, dr, dz, dc, u * on

    def kinds_ext(kinds):
        row = iota((16, ROWS), 0)
        return jnp.where(jnp.logical_or(row == kinds, row == 8), 1.0, 0.0).astype(BF16)

    def grads(s, factors):
        a, b, c, d, u = factors
        dr = (s * b).astype(BF16)
        dz = (s * c).astype(BF16)
        dc = (s * d).astype(BF16)
        dn = (s * a).astype(BF16)
        down = (
            s * u
            + dot_nt(dr, w[:, :H])
            + dot_nt(dz, w[:, H : 2 * H])
            + dot_nt(dc, w[:, 2 * H :])
        )
        return dr, dz, dc, dn, down.astype(BF16)

    wacc[...] = jnp.zeros_like(wacc)
    eacc[...] = jnp.zeros_like(eacc)

    def level_one(c):
        m = msg1[c]
        kinds = types[c, 1:2, :]
        factors = coefficients(m, kinds, me * ROWS, live[1, c])
        dr, dz, dc, dn, down = grads(sg1[c].astype(F32), factors)
        dm_s[c] = down
        ext = kinds_ext(kinds)
        for i, g in enumerate((dr, dz, dc)):
            wacc[:, i * H : (i + 1) * H] += dot_tn(m, g)
        for i, g in enumerate((dr, dz, dc, dn)):
            eacc[:, i * H : (i + 1) * H] += dot_nn(ext, g)

    load_m.wait()
    load_s.wait()
    each(CIRC, level_one)

    pl.semaphore_wait(barrier, 8 + rows_y - 1 + rows_x - 1 + 2)
    each(
        rows_x - 1,
        lambda i: pl.semaphore_signal(
            plane_ready,
            inc=1,
            device_id={"band": lax.rem(bx + 1 + i, rows_x) * rows_y + by},
            device_id_type=pl.DeviceIdType.MESH,
        ),
    )
    for b in (beside_y, beside_x)[: min(rows_x, 2)]:
        pl.semaphore_signal(
            pair_ready, inc=1, device_id={"band": b}, device_id_type=pl.DeviceIdType.MESH
        )

    @pl.when(band < bands - 1)
    def _():
        pl.semaphore_signal(
            below_ready,
            inc=1,
            device_id={"band": jnp.minimum(band + 1, bands - 1)},
            device_id_type=pl.DeviceIdType.MESH,
        )

    def block(k):
        return pl.ds(pl.multiple_of(k * ROWS, ROWS), ROWS)

    def half_block(k, e):
        return pl.ds(pl.multiple_of(k * ROWS + e * (ROWS // 2), ROWS // 2), ROWS // 2)

    def steps_to(c):
        return lax.rem(2 * c + parity + 8 - z, 8)

    def gate_of(c):
        return 2 * (2 * c + parity) + half

    top, bottom = pl.ds(0, ROWS // 2), pl.ds(ROWS // 2, ROWS // 2)

    def to_task(src_of, buf, base, ssem, rsem):
        for c in range(CIRC):
            steps = steps_to(c)

            @pl.when(steps == 0)
            def _():
                pltpu.make_async_copy(src_of(c), buf.at[block(base + z)], rsem.at[z]).start()

            @pl.when(steps == 4)
            def _():
                send(
                    src_of(c).at[top],
                    buf.at[half_block(base + z, 0)],
                    ssem,
                    rsem.at[z],
                    gate=gate_of(c),
                )

            @pl.when(
                jnp.logical_and(
                    jnp.logical_and(steps != 0, steps != 4),
                    jnp.logical_and(steps != 1, steps != 7),
                )
            )
            def _():
                send(src_of(c), buf.at[block(base + z)], ssem, rsem.at[z], gate=gate_of(c))

    def to_task_by(src_of, buf, base, ssem, rsem):
        for c in range(CIRC):
            steps = steps_to(c)

            @pl.when(steps == 1)
            def _():
                send(
                    src_of(c),
                    buf.at[block(base + z)],
                    ssem,
                    rsem.at[z],
                    gate=gate_of(c),
                    to_band=beside_y,
                )

            @pl.when(steps == 4)
            def _():
                send(
                    src_of(c).at[bottom],
                    buf.at[half_block(base + z, 1)],
                    ssem,
                    rsem.at[z],
                    gate=gate_of(c),
                    to_band=beside_y,
                )

            @pl.when(steps == 7)
            def _():
                send(
                    src_of(c),
                    buf.at[block(base + z)],
                    ssem,
                    rsem.at[z],
                    gate=gate_of(c),
                    to_band=beside_x,
                )

    def hand_on(buf, base, ssem, rsem):
        for steps, b in ((1, beside_y), (7, beside_x), (4, beside_y)):
            k = lax.rem(z + 8 - steps, 8)
            place = half_block(base + k, 1) if steps == 4 else block(base + k)
            wait(buf.at[0 : ROWS // 2] if steps == 4 else buf.at[0:ROWS], rsem.at[k])
            send(buf.at[place], buf.at[place], ssem, rsem.at[k], to_band=b)

    for c in range(CIRC):

        @pl.when(steps_to(c) == 0)
        def _():
            idx_r[half, z] = idx_s[c]

        @pl.when(steps_to(c) != 0)
        def _():
            send(idx_s.at[c], idx_r.at[half, z], sem_s.at[0], idx_sem, gate=gate_of(c))

    first_units = (
        (lambda c: dm_s.at[c], d1, 8 * half, sem_s.at[3], dm_sem),
        (lambda c: msg.at[c, 0], m0, 0, sem_s.at[1], m0_sem),
        (lambda c: sg.at[c, 0], sg0, 0, sem_s.at[2], sg0_sem),
    )
    last_unit = (lambda c: msg1.at[c], m1, 0, sem_s.at[4], m1_sem)
    to_task(*first_units[0])
    pl.semaphore_wait(pair_ready, min(rows_x, 2))
    to_task_by(*first_units[0])
    for unit in first_units[1:]:
        to_task_by(*unit)
        to_task(*unit)
    py, px = 8 // rows_y, 4 // rows_x

    def x_part(ref, x):
        return ref.at[pl.ds(x * px, px)]

    def piece_of(ref, to):
        return ref.at[pl.ds((to // rows_y) * px, px), pl.ds(lax.rem(to, rows_y) * py, py)]

    if rows_y == 8:
        flat = half == 0
        place = jnp.where(flat, band, bx * rows_y + z)
        height = jnp.where(flat, z, by)
    else:
        flat = half >= 0
        place, height = band, z

    def send_in_plane(src, dst, ssem, rsem, to):
        send(
            src,
            dst,
            ssem,
            rsem,
            gate=jnp.where(flat, me, 2 * lax.rem(to, rows_y) + half),
            to_band=jnp.where(flat, to, (to // rows_y) * rows_y + by),
        )

    def send_across(src, dst, ssem, rsem, to):
        send(
            src,
            dst,
            ssem,
            rsem,
            gate=jnp.where(flat, 2 * to + half, me),
            to_band=jnp.where(flat, band, bx * rows_y + lax.rem(to, rows_y)),
        )

    def halve():
        for i in range(GATES):
            for n in range(3):
                half_s[i % 2, n, i // 2] = wacc[16 * i : 16 * i + 16, n * H : (n + 1) * H].astype(
                    BF16
                )
            if i < 4:
                half_s[i % 2, 3, i // 2] = eacc[:, i * H : (i + 1) * H].astype(BF16)
            else:
                half_s[i % 2, 3, i // 2] = jnp.zeros((16, H), BF16)
        send(half_s.at[1 - half], half_r, sem_s.at[5], wr_sem.at[0], gate=sibling)

    def over_plane():
        wait(half_r, wr_sem.at[0])
        for n in range(4):
            plane_s[n] = (half_s[half, n].astype(F32) + half_r[n].astype(F32)).astype(BF16)
        pl.semaphore_wait(plane_ready, rows_x - 1)

        def to(i):
            peer = lax.rem(place + 1 + i, bands)
            send_in_plane(
                piece_of(plane_s, peer), plane_r.at[place], sem_s.at[11], wr_sem.at[1], peer
            )

        each(bands - 1, to)
        plane_r[place] = piece_of(plane_s, place)[...]

    def along_ring():
        wait(plane_r.at[0 : bands - 1], wr_sem.at[1])
        total = plane_r[0].astype(F32)
        for i in range(1, bands):
            total = total + plane_r[i].astype(F32)
        z_r[height] = total.astype(BF16)

        def to(i):
            peer = lax.rem(height + 1 + i, 8)
            send_across(z_r.at[height], z_r.at[height], sem_s.at[15], wr_sem.at[4], peer)

        each(7, to)

    def late():
        to_task(*last_unit)
        to_task_by(*last_unit)

    def turn(t):
        off = jnp.where(lax.rem(t, 2) == 1, (t + 1) // 2, 8 - t // 2)
        return lax.rem(z + off, 8)

    @pl.when(active)
    def _():
        wait(idx_r.at[0, 0:7], idx_sem)
        send(idx_r.at[half], idx_r.at[half], sem_s.at[18], fi_sem, gate=sibling)

        def build(j):
            tile = idx_r[j // 8, lax.rem(j, 8)]
            col = pl.ds(pl.multiple_of(j * ROWS, ROWS), ROWS)
            spot = iota((ROWS, ROWS), 0)
            block = 2 * iota((8, ROWS), 0) + half
            for lv in (1, 0):
                at = jnp.full((8, ROWS), -1, jnp.int32)
                for f in range(4):
                    t = tile[4 * lv + f : 4 * lv + f + 1, :]
                    at = jnp.where(
                        lax.shift_right_logical(t, 7) == block, lax.bitwise_and(t, 127), at
                    )
                for k in range(8):
                    sel[lv, k * ROWS : (k + 1) * ROWS, col] = jnp.where(
                        spot == at[k : k + 1, :], 1.0, 0.0
                    ).astype(BF16)

        each(8, lambda k: build(8 * half + k))
        wait(idx_r.at[0], fi_sem)
        each(8, lambda k: build(8 - 8 * half + k))

        def forward(lv, m_ref, sem):
            def step(t):
                k = turn(t)

                wait(m_ref.at[0:ROWS], sem.at[k])
                rows = pl.ds(pl.multiple_of(k * ROWS, ROWS), ROWS)
                j = 2 * k + half
                kinds = idx_r[half, k, 8 + lv : 9 + lv, :]
                factors = coefficients(m_ref[rows], kinds, j * ROWS, live[lv, mine])
                for i, f in enumerate(factors):
                    coef[lv, i, rows] = f
                xts[lv, :, rows] = kinds_ext(kinds)

            each(8, step)

        forward(0, m0, m0_sem)
        for i in range(1, 4):
            wait(m0.at[0 : 3 * ROWS], sem_s.at[i])
        late()

        def relay(t):
            k = turn(t)
            rows = pl.ds(pl.multiple_of(half * OWN + k * ROWS, ROWS), ROWS)

            wait(d1.at[0:ROWS], dm_sem.at[k])
            send(d1.at[rows], d1.at[rows], sem_s.at[6], fw_sem, gate=sibling)

        each(8, relay)
        each(8, lambda i: wait(sg0.at[0:ROWS], sg0_sem.at[i]))
        wait(d1.at[0:OWN], fw_sem)

        def chunk(n):
            return pl.ds(pl.multiple_of(n * CHUNK, CHUNK), CHUNK)

        def backward(lv, s, n, dst, sem, ssem):
            rows = chunk(n)
            factors = tuple(coef[lv, i, rows] for i in range(5))
            dr, dz, dc, dn, down = grads(s, factors)
            for i, g in enumerate((dr, dz, dc, dn)):
                gbuf[rows, i * H : (i + 1) * H] = g
            place = pl.ds(pl.multiple_of(half * OWN + n * CHUNK, CHUNK), CHUNK)
            dst[place] = down
            send(dst.at[place], dst.at[place], ssem, sem, gate=sibling)

        def collect(lv, n, src):
            return dot_nn(sel[lv, chunk(n)], src[...])

        @pl.when(band > 0)
        def _():
            pl.semaphore_wait(below_ready, 1)

        def first_zero(n):
            s = sg0[chunk(n)].astype(F32) + collect(1, n, d1)
            s0[chunk(n)] = s
            backward(0, s, n, d2, ex_sem.at[0], sem_s.at[7])

        each(NCH, first_zero)
        wait(d2.at[0:OWN], ex_sem.at[0])

        def first_out(n):
            rows = chunk(n)
            q_s[rows] = collect(0, n, d2).astype(BF16)

            @pl.when(band > 0)
            def _():
                def part(e):
                    i = n * (CHUNK // PART) + e
                    place = pl.ds(pl.multiple_of(i * PART, PART), PART)

                    @pl.when(i < DETOUR // PART)
                    def _():
                        send(
                            q_s.at[place],
                            q_r.at[place],
                            sem_s.at[8],
                            qp_sem.at[i],
                            gate=2 * (2 * mine + 1 - parity) + half,
                        )

                    @pl.when(i >= DETOUR // PART)
                    def _():
                        send(
                            q_s.at[place],
                            q_r.at[place],
                            sem_s.at[8],
                            q_sem.at[n],
                            gate=2 * (2 * mine + below_parity) + half,
                            to_band=below,
                        )

                each(CHUNK // PART, part)

            @pl.when(band == bands - 1)
            def _():
                q_r[rows] = jnp.zeros((CHUNK, H), BF16)

        each(NCH, first_out)
        forward(1, m1, m1_sem)

        def second_one(n):
            @pl.when(band < bands - 1)
            def _():
                wait(q_r.at[0:CHUNK], q_sem.at[n])

            backward(1, q_r[chunk(n)].astype(F32), n, d3, ex_sem.at[1], sem_s.at[9])

        each(NCH, second_one)

        for i in range(3):
            wacc[:, i * H : (i + 1) * H] += dot_tn(m1[...], gbuf[:, i * H : (i + 1) * H])
        for i in range(4):
            eacc[:, i * H : (i + 1) * H] += dot_nn(xts[1], gbuf[:, i * H : (i + 1) * H])
        wait(d3.at[0:OWN], ex_sem.at[1])

        def second_zero(n):
            s = s0[chunk(n)] + collect(1, n, d3)
            backward(0, s, n, d4, ex_sem.at[2], sem_s.at[10])

        each(NCH, second_zero)
        for i in range(3):
            wacc[:, i * H : (i + 1) * H] += dot_tn(m0[...], gbuf[:, i * H : (i + 1) * H])
        for i in range(4):
            eacc[:, i * H : (i + 1) * H] += dot_nn(xts[0], gbuf[:, i * H : (i + 1) * H])
        halve()

        wait(d4.at[0:OWN], ex_sem.at[2])

        @pl.when(band > 0)
        def _():
            wait(q_s, sem_s.at[8])

        def second_out(n):
            q_s[chunk(n)] = collect(0, n, d4).astype(BF16)

        def deliver(k):
            @pl.when(k == z)
            def _():
                out[mine] = q_s[block(k)]

            @pl.when(k != z)
            def _():
                send(q_s.at[block(k)], out.at[mine], sem_s.at[12], out_sem, gate=2 * k + half)

        over_plane()
        each(NCH // 2, second_out)
        each(NCH // 2, lambda n: second_out(NCH // 2 + n))
        along_ring()
        each(8, deliver)

    @pl.when(jnp.logical_not(active))
    def _():
        for _, buf, base, ssem, rsem in first_units:
            hand_on(buf, base, ssem, rsem)
        for i in range(1, 4):
            wait(m0.at[0 : 4 * ROWS + PASSED], sem_s.at[i])
        late()
        hand_on(*last_unit[1:])

        @pl.when(band > 0)
        def _():
            def pass_on(i):
                place = pl.ds(pl.multiple_of(i * PART, PART), PART)
                wait(q_r.at[0:PART], qp_sem.at[i])
                send(
                    q_r.at[place],
                    q_r.at[place],
                    sem_s.at[8],
                    q_sem.at[i // (CHUNK // PART)],
                    gate=2 * (2 * mine + below_parity) + half,
                    to_band=below,
                )

            pl.semaphore_wait(below_ready, 1)
            each(DETOUR // PART, pass_on)

        halve()
        over_plane()
        along_ring()

    wait(z_r.at[0:7], wr_sem.at[4])
    total = z_r[0].astype(F32)
    for i in range(1, 8):
        total = total + z_r[i].astype(F32)
    total = total * (1.0 / math.sqrt(CIRC * bands * 2 * ROWS * GATES))
    done = piece_of(summed.at[half], place)
    done[...] = total.astype(BF16)

    def to_plane(i):
        peer = lax.rem(place + 1 + i, bands)
        send_in_plane(done, done, sem_s.at[16], ax_sem.at[bx], peer)

    each(bands - 1, to_plane)

    def to_sibling(i):
        x = lax.rem(bx + i, rows_x)
        there = x_part(summed.at[half], x)

        @pl.when(i == 0)
        def _():
            wait(plane_r.at[0 : rows_y - 1], ax_sem.at[x])

        @pl.when(i > 0)
        def _():
            wait(plane_r.at[0:rows_y], ax_sem.at[x])

        send(there, there, sem_s.at[17], wr_sem.at[6], gate=sibling)

    each(rows_x, to_sibling)
    wait(summed.at[half], wr_sem.at[6])

    @pl.when(active)
    def _():
        wait(out.at[0:3], out_sem)
        wait(idx_r.at[0, 0:3], sem_s.at[0])
        wait(idx_r.at[0], sem_s.at[18])
        wait(m0.at[0 : 3 * ROWS], sem_s.at[4])
        wait(d1.at[0:OWN], sem_s.at[6])
        wait(d1.at[0:OWN], sem_s.at[7])
        wait(d1.at[0:OWN], sem_s.at[9])
        wait(d1.at[0:OWN], sem_s.at[10])
        wait(q_s.at[0 : 7 * ROWS], sem_s.at[12])

    @pl.when(jnp.logical_not(active))
    def _():
        wait(out, out_sem)
        wait(idx_r.at[0, 0:4], sem_s.at[0])
        wait(m0.at[0 : 4 * ROWS + PASSED], sem_s.at[4])

        @pl.when(band > 0)
        def _():
            wait(q_r.at[0:DETOUR], sem_s.at[8])

    wait(half_r, sem_s.at[5])
    wait(plane_r.at[0 : bands - 1], sem_s.at[11])
    wait(z_r.at[0:7], sem_s.at[15])
    wait(plane_r.at[0 : bands - 1], sem_s.at[16])
    wait(summed.at[half], sem_s.at[17])


def finish_body(moved, summed, out, wout, bout, tout):
    out[...] = moved[...]
    for s in range(GATES):
        for n in range(3):
            wout[16 * s : 16 * s + 16, n * H : (n + 1) * H] = summed[s % 2, n, s // 2].astype(F32)
    for s in range(4):
        ext = summed[s % 2, 3, s // 2].astype(F32)
        if s != 2:
            n = min(s, 2)
            tout[:, n * H : (n + 1) * H] = ext[:8]
        if s < 3:
            bout[s * H : (s + 1) * H] = ext[8]


def shards(
    messages,
    gate_type,
    state_grad,
    fanin_owner,
    fanin_slot,
    live_count,
    hidden_weight,
    hidden_bias,
    type_table,
):
    bands = lax.axis_size("band")
    cols = min(8, bands)
    rows_x = bands // cols
    py, px = 8 // cols, 4 // rows_x
    owners = jnp.swapaxes(fanin_owner[:, 0], 2, 3)
    slots = jnp.swapaxes(fanin_slot[:, 0], 2, 3)
    vmem = pl.BlockSpec(memory_space=pltpu.VMEM)
    hbm = pl.BlockSpec(memory_space=pl.ANY)
    dma = pltpu.SemaphoreType.DMA

    def body(*refs):
        kernel_body(bands, cols, *refs)

    moved, summed = pl.pallas_call(
        body,
        out_shape=(
            jax.ShapeDtypeStruct((CIRC, ROWS, H), BF16),
            jax.ShapeDtypeStruct((2,) + PIECES, BF16),
        ),
        in_specs=[hbm, vmem, hbm, vmem, vmem, pl.BlockSpec(memory_space=pltpu.SMEM)] + [vmem] * 3,
        out_specs=(vmem, vmem),
        scratch_shapes=[
            pltpu.VMEM((CIRC, 16, ROWS), jnp.int32),
            pltpu.VMEM((2, 8, 16, ROWS), jnp.int32),
            pltpu.VMEM((32, 3 * H), BF16),
            pltpu.VMEM((OWN, H), BF16),
            pltpu.VMEM((OWN, H), BF16),
            pltpu.VMEM((OWN, H), BF16),
            pltpu.VMEM((CIRC, ROWS, H), BF16),
            pltpu.VMEM((2 * OWN, H), BF16),
            pltpu.VMEM((2 * OWN, H), BF16),
            pltpu.VMEM((2 * OWN, H), BF16),
            pltpu.VMEM((2 * OWN, H), BF16),
            pltpu.VMEM((2, OWN, 2 * OWN), BF16),
            pltpu.VMEM((2, 5, OWN, H), F32),
            pltpu.VMEM((2, 16, OWN), BF16),
            pltpu.VMEM((OWN, H), F32),
            pltpu.VMEM((OWN, 4 * H), BF16),
            pltpu.VMEM((OWN, H), BF16),
            pltpu.VMEM((OWN, H), BF16),
            pltpu.VMEM((H, 3 * H), F32),
            pltpu.VMEM((16, 4 * H), F32),
            pltpu.VMEM((CIRC, ROWS, H), BF16),
            pltpu.VMEM((CIRC, ROWS, H), BF16),
            pltpu.VMEM((2,) + PIECES, BF16),
            pltpu.VMEM(PIECES, BF16),
            pltpu.VMEM(PIECES, BF16),
            pltpu.VMEM((bands, px, py, 16, H), BF16),
            pltpu.VMEM((8, px, py, 16, H), BF16),
            dma((19,)),
            dma,
            dma,
            dma((8,)),
            dma((8,)),
            dma((8,)),
            dma((8,)),
            dma,
            dma((3,)),
            dma((NCH,)),
            dma((DETOUR // PART,)),
            dma,
            dma((7,)),
            dma((rows_x,)),
            dma((2,)),
            pltpu.SemaphoreType.REGULAR,
            pltpu.SemaphoreType.REGULAR,
            pltpu.SemaphoreType.REGULAR,
        ],
        compiler_params=pltpu.CompilerParams(
            collective_id=0, has_side_effects=True, vmem_limit_bytes=56 * 1024 * 1024
        ),
        name="band_passes",
    )(
        messages[:, 0],
        gate_type[:, 0],
        state_grad[:, 0],
        owners,
        slots,
        live_count[:, 0].T,
        hidden_weight,
        hidden_bias,
        type_table,
    )
    out, weight, bias, rows = pl.pallas_call(
        finish_body,
        out_shape=(
            jax.ShapeDtypeStruct((CIRC, ROWS, H), BF16),
            jax.ShapeDtypeStruct((H, 3 * H), F32),
            jax.ShapeDtypeStruct((3 * H,), F32),
            jax.ShapeDtypeStruct((8, 3 * H), F32),
        ),
        in_specs=[vmem] * 2,
        out_specs=(vmem,) * 4,
        name="results",
    )(moved, summed)
    return out[:, None], weight, bias, rows


def solution(mesh):
    return jax.shard_map(
        shards,
        mesh=mesh,
        in_specs=(
            P(None, "band", None, "gate", None),
            P(None, "band", None, "gate"),
            P(None, "band", None, "gate", None),
            P(None, "band", None, "gate", None),
            P(None, "band", None, "gate", None),
            P(None, "band", None),
            P(),
            P(),
            P(),
        ),
        out_specs=(P(None, "band", "gate", None), P(), P(), P()),
        check_vma=False,
    )
```

```python
import math

import jax
import jax.numpy as jnp
from jax import lax
from jax.experimental import pallas as pl
from jax.experimental.pallas import tpu as pltpu
from jax.sharding import PartitionSpec as P

F32 = jnp.float32
BF16 = jnp.bfloat16
H = 256
ROWS = 128
GATES = 16
CIRC = 4
OWN = 1024
CHUNK = 256
NCH = OWN // CHUNK
PART = 64
PASSED = 5 * ROWS // 2
DETOUR = 320
PIECES = (4, 8, 16, H)


def iota(shape, dim):
    return lax.broadcasted_iota(jnp.int32, shape, dim)


def dot_tn(a, b):
    return lax.dot_general(a, b, (((0,), (0,)), ((), ())), preferred_element_type=F32)


def dot_nt(a, b):
    return lax.dot_general(a, b, (((1,), (1,)), ((), ())), preferred_element_type=F32)


def dot_nn(a, b):
    return jnp.dot(a, b, preferred_element_type=F32)


def kernel_body(
    bands,
    cols,
    msg,
    types,
    sg,
    owner,
    slot,
    live,
    w,
    bias,
    table,
    out,
    summed,
    idx_s,
    idx_r,
    pieces,
    m0,
    sg0,
    m1,
    dm_s,
    d1,
    d2,
    d3,
    d4,
    sel,
    coef,
    xts,
    s0,
    gbuf,
    q_s,
    q_r,
    wacc,
    eacc,
    msg1,
    sg1,
    half_s,
    half_r,
    plane_s,
    plane_r,
    z_r,
    sem_s,
    idx_sem,
    fi_sem,
    m0_sem,
    sg0_sem,
    dm_sem,
    m1_sem,
    fw_sem,
    ex_sem,
    q_sem,
    qp_sem,
    out_sem,
    wr_sem,
    ax_sem,
    own_sem,
    pair_ready,
    below_ready,
    plane_ready,
):
    rows_y = cols
    rows_x = bands // cols
    me = lax.axis_index("gate")
    band = lax.axis_index("band")
    z = me // 2
    half = lax.rem(me, 2)
    mine = z // 2
    sibling = me + 1 - 2 * half
    by = lax.rem(band, rows_y)
    bx = band // rows_y

    def parity_of(b):
        return lax.rem(b + b // rows_y, 2)

    parity = parity_of(band)
    active = lax.rem(z, 2) == parity
    below = jnp.maximum(band - 1, 0)
    below_parity = parity_of(below)
    beside_y = bx * rows_y + by + 1 - 2 * lax.rem(by, 2)
    beside_x = (bx + 1 - 2 * lax.rem(bx, 2)) * rows_y + by if rows_x > 1 else beside_y

    def send(src, dst, ssem, rsem, gate=None, to_band=None):
        where = {}
        if to_band is not None:
            where["band"] = to_band
        if gate is not None:
            where["gate"] = gate
        pltpu.make_async_remote_copy(
            src_ref=src,
            dst_ref=dst,
            send_sem=ssem,
            recv_sem=rsem,
            device_id=where,
            device_id_type=pl.DeviceIdType.MESH,
        ).start()

    def wait(ref, sem):
        pltpu.make_async_copy(ref, ref, sem).wait()

    def each(count, body):
        def step(i, carry):
            body(i)
            return carry

        lax.fori_loop(0, count, step, 0)

    load_m = pltpu.make_async_copy(msg.at[:, 1], msg1, own_sem.at[0])
    load_s = pltpu.make_async_copy(sg.at[:, 1], sg1, own_sem.at[1])
    load_m.start()
    load_s.start()

    barrier = pltpu.get_barrier_semaphore()

    def greet(**where):
        pl.semaphore_signal(
            barrier, inc=1, device_id=where, device_id_type=pl.DeviceIdType.MESH
        )

    each(7, lambda i: greet(gate=lax.rem(me + 2 + 2 * i, GATES)))
    greet(gate=sibling)
    each(rows_y - 1, lambda i: greet(band=bx * rows_y + lax.rem(by + 1 + i, rows_y)))
    if rows_x > 1:
        each(rows_x - 1, lambda i: greet(band=lax.rem(bx + 1 + i, rows_x) * rows_y + by))
    greet(band=lax.rem(band + 1, bands))
    greet(band=lax.rem(band + bands - 1, bands))

    for c in range(CIRC):
        for lv in range(2):
            idx_s[c, 4 * lv : 4 * lv + 4, :] = owner[c, lv] * ROWS + slot[c, lv]
        idx_s[c, 8:10, :] = types[c]
        idx_s[c, 10:16, :] = jnp.zeros((6, ROWS), jnp.int32)
    full_bias = bias[...].reshape(1, 3 * H)
    full = table[...] + jnp.where(iota((8, 3 * H), 1) < 2 * H, full_bias, 0.0)
    hi = full.astype(BF16)
    rest = full - hi.astype(F32)
    mid = rest.astype(BF16)
    low = (rest - mid.astype(F32)).astype(BF16)
    pieces[...] = jnp.concatenate(
        [hi.astype(F32), mid.astype(F32), low.astype(F32), jnp.zeros((8, 3 * H), F32)], axis=0
    ).astype(BF16)
    cand_bias = full_bias[:, 2 * H :]

    def coefficients(m, kinds, gate0, count):
        hot = jnp.where(lax.bitwise_and(iota((32, ROWS), 0), 7) == kinds, 1.0, 0.0).astype(BF16)
        inp = dot_tn(hot, pieces[...])
        pre = dot_nn(m, w[...])
        tr = jnp.tanh(0.5 * (inp[:, :H] + pre[:, :H]))
        tu = jnp.tanh(0.5 * (inp[:, H : 2 * H] + pre[:, H : 2 * H]))
        cand = pre[:, 2 * H :] + cand_bias
        r = 0.5 + 0.5 * tr
        u = 0.5 + 0.5 * tu
        new = jnp.tanh(inp[:, 2 * H :] + r * cand)
        on = jnp.where(iota((ROWS, 1), 0) + gate0 < count, 1.0, 0.0)
        a = (1.0 - u) * (1.0 - new * new) * on
        dc = a * r
        dr = a * cand * (r * (1.0 - r))
        dz = (m.astype(F32) - new) * (u * (1.0 - u)) * on
        return a, dr, dz, dc, u * on

    def kinds_ext(kinds):
        row = iota((16, ROWS), 0)
        return jnp.where(jnp.logical_or(row == kinds, row == 8), 1.0, 0.0).astype(BF16)

    def grads(s, factors):
        a, b, c, d, u = factors
        dr = (s * b).astype(BF16)
        dz = (s * c).astype(BF16)
        dc = (s * d).astype(BF16)
        dn = (s * a).astype(BF16)
        down = (
            s * u
            + dot_nt(dr, w[:, :H])
            + dot_nt(dz, w[:, H : 2 * H])
            + dot_nt(dc, w[:, 2 * H :])
        )
        return dr, dz, dc, dn, down.astype(BF16)

    wacc[...] = jnp.zeros_like(wacc)
    eacc[...] = jnp.zeros_like(eacc)

    def level_one(c):
        m = msg1[c]
        kinds = types[c, 1:2, :]
        factors = coefficients(m, kinds, me * ROWS, live[1, c])
        dr, dz, dc, dn, down = grads(sg1[c].astype(F32), factors)
        dm_s[c] = down
        ext = kinds_ext(kinds)
        for i, g in enumerate((dr, dz, dc)):
            wacc[:, i * H : (i + 1) * H] += dot_tn(m, g)
        for i, g in enumerate((dr, dz, dc, dn)):
            eacc[:, i * H : (i + 1) * H] += dot_nn(ext, g)

    load_m.wait()
    load_s.wait()
    each(CIRC, level_one)

    pl.semaphore_wait(barrier, 8 + rows_y - 1 + rows_x - 1 + 2)
    each(
        rows_x - 1,
        lambda i: pl.semaphore_signal(
            plane_ready,
            inc=1,
            device_id={"band": lax.rem(bx + 1 + i, rows_x) * rows_y + by},
            device_id_type=pl.DeviceIdType.MESH,
        ),
    )
    for b in (beside_y, beside_x)[: min(rows_x, 2)]:
        pl.semaphore_signal(
            pair_ready, inc=1, device_id={"band": b}, device_id_type=pl.DeviceIdType.MESH
        )

    @pl.when(band < bands - 1)
    def _():
        pl.semaphore_signal(
            below_ready,
            inc=1,
            device_id={"band": jnp.minimum(band + 1, bands - 1)},
            device_id_type=pl.DeviceIdType.MESH,
        )

    def block(k):
        return pl.ds(pl.multiple_of(k * ROWS, ROWS), ROWS)

    def half_block(k, e):
        return pl.ds(pl.multiple_of(k * ROWS + e * (ROWS // 2), ROWS // 2), ROWS // 2)

    def steps_to(c):
        return lax.rem(2 * c + parity + 8 - z, 8)

    def gate_of(c):
        return 2 * (2 * c + parity) + half

    top, bottom = pl.ds(0, ROWS // 2), pl.ds(ROWS // 2, ROWS // 2)

    def to_task(src_of, buf, base, ssem, rsem):
        for c in range(CIRC):
            steps = steps_to(c)

            @pl.when(steps == 0)
            def _():
                pltpu.make_async_copy(src_of(c), buf.at[block(base + z)], rsem.at[z]).start()

            @pl.when(steps == 4)
            def _():
                send(
                    src_of(c).at[top],
                    buf.at[half_block(base + z, 0)],
                    ssem,
                    rsem.at[z],
                    gate=gate_of(c),
                )

            @pl.when(
                jnp.logical_and(
                    jnp.logical_and(steps != 0, steps != 4),
                    jnp.logical_and(steps != 1, steps != 7),
                )
            )
            def _():
                send(src_of(c), buf.at[block(base + z)], ssem, rsem.at[z], gate=gate_of(c))

    def to_task_by(src_of, buf, base, ssem, rsem):
        for c in range(CIRC):
            steps = steps_to(c)

            @pl.when(steps == 1)
            def _():
                send(
                    src_of(c),
                    buf.at[block(base + z)],
                    ssem,
                    rsem.at[z],
                    gate=gate_of(c),
                    to_band=beside_y,
                )

            @pl.when(steps == 4)
            def _():
                send(
                    src_of(c).at[bottom],
                    buf.at[half_block(base + z, 1)],
                    ssem,
                    rsem.at[z],
                    gate=gate_of(c),
                    to_band=beside_y,
                )

            @pl.when(steps == 7)
            def _():
                send(
                    src_of(c),
                    buf.at[block(base + z)],
                    ssem,
                    rsem.at[z],
                    gate=gate_of(c),
                    to_band=beside_x,
                )

    def hand_on(buf, base, ssem, rsem):
        for steps, b in ((1, beside_y), (7, beside_x), (4, beside_y)):
            k = lax.rem(z + 8 - steps, 8)
            place = half_block(base + k, 1) if steps == 4 else block(base + k)
            wait(buf.at[0 : ROWS // 2] if steps == 4 else buf.at[0:ROWS], rsem.at[k])
            send(buf.at[place], buf.at[place], ssem, rsem.at[k], to_band=b)

    for c in range(CIRC):

        @pl.when(steps_to(c) == 0)
        def _():
            idx_r[half, z] = idx_s[c]

        @pl.when(steps_to(c) != 0)
        def _():
            send(idx_s.at[c], idx_r.at[half, z], sem_s.at[0], idx_sem, gate=gate_of(c))

    first_units = (
        (lambda c: dm_s.at[c], d1, 8 * half, sem_s.at[3], dm_sem),
        (lambda c: msg.at[c, 0], m0, 0, sem_s.at[1], m0_sem),
        (lambda c: sg.at[c, 0], sg0, 0, sem_s.at[2], sg0_sem),
    )
    last_unit = (lambda c: msg1.at[c], m1, 0, sem_s.at[4], m1_sem)
    to_task(*first_units[0])
    pl.semaphore_wait(pair_ready, min(rows_x, 2))
    to_task_by(*first_units[0])
    for unit in first_units[1:]:
        to_task_by(*unit)
        to_task(*unit)
    py, px = 8 // rows_y, 4 // rows_x

    def x_part(ref, x):
        return ref.at[pl.ds(x * px, px)]

    def piece_of(ref, to):
        return ref.at[pl.ds((to // rows_y) * px, px), pl.ds(lax.rem(to, rows_y) * py, py)]

    if rows_y == 8:
        flat = half == 0
        place = jnp.where(flat, band, bx * rows_y + z)
        height = jnp.where(flat, z, by)
    else:
        flat = half >= 0
        place, height = band, z

    def send_in_plane(src, dst, ssem, rsem, to):
        send(
            src,
            dst,
            ssem,
            rsem,
            gate=jnp.where(flat, me, 2 * lax.rem(to, rows_y) + half),
            to_band=jnp.where(flat, to, (to // rows_y) * rows_y + by),
        )

    def send_across(src, dst, ssem, rsem, to):
        send(
            src,
            dst,
            ssem,
            rsem,
            gate=jnp.where(flat, 2 * to + half, me),
            to_band=jnp.where(flat, band, bx * rows_y + lax.rem(to, rows_y)),
        )

    def halve():
        for i in range(GATES):
            for n in range(3):
                half_s[i % 2, n, i // 2] = wacc[16 * i : 16 * i + 16, n * H : (n + 1) * H].astype(
                    BF16
                )
            if i < 4:
                half_s[i % 2, 3, i // 2] = eacc[:, i * H : (i + 1) * H].astype(BF16)
            else:
                half_s[i % 2, 3, i // 2] = jnp.zeros((16, H), BF16)
        send(half_s.at[1 - half], half_r, sem_s.at[5], wr_sem.at[0], gate=sibling)

    def over_plane():
        wait(half_r, wr_sem.at[0])
        for n in range(4):
            plane_s[n] = (half_s[half, n].astype(F32) + half_r[n].astype(F32)).astype(BF16)
        pl.semaphore_wait(plane_ready, rows_x - 1)

        def to(i):
            peer = lax.rem(place + 1 + i, bands)
            send_in_plane(
                piece_of(plane_s, peer), plane_r.at[place], sem_s.at[11], wr_sem.at[1], peer
            )

        each(bands - 1, to)
        plane_r[place] = piece_of(plane_s, place)[...]

    def along_ring():
        wait(plane_r.at[0 : bands - 1], wr_sem.at[1])
        total = plane_r[0].astype(F32)
        for i in range(1, bands):
            total = total + plane_r[i].astype(F32)
        z_r[height] = total.astype(BF16)

        def to(i):
            peer = lax.rem(height + 1 + i, 8)
            send_across(z_r.at[height], z_r.at[height], sem_s.at[15], wr_sem.at[4], peer)

        each(7, to)

    def late():
        to_task(*last_unit)
        to_task_by(*last_unit)

    def turn(t):
        off = jnp.where(lax.rem(t, 2) == 1, (t + 1) // 2, 8 - t // 2)
        return lax.rem(z + off, 8)

    @pl.when(active)
    def _():
        wait(idx_r.at[0, 0:7], idx_sem)
        send(idx_r.at[half], idx_r.at[half], sem_s.at[18], fi_sem, gate=sibling)

        def build(j):
            tile = idx_r[j // 8, lax.rem(j, 8)]
            col = pl.ds(pl.multiple_of(j * ROWS, ROWS), ROWS)
            spot = iota((ROWS, ROWS), 0)
            block = 2 * iota((8, ROWS), 0) + half
            for lv in (1, 0):
                at = jnp.full((8, ROWS), -1, jnp.int32)
                for f in range(4):
                    t = tile[4 * lv + f : 4 * lv + f + 1, :]
                    at = jnp.where(
                        lax.shift_right_logical(t, 7) == block, lax.bitwise_and(t, 127), at
                    )
                for k in range(8):
                    sel[lv, k * ROWS : (k + 1) * ROWS, col] = jnp.where(
                        spot == at[k : k + 1, :], 1.0, 0.0
                    ).astype(BF16)

        each(8, lambda k: build(8 * half + k))
        wait(idx_r.at[0], fi_sem)
        each(8, lambda k: build(8 - 8 * half + k))

        def forward(lv, m_ref, sem):
            def step(t):
                k = turn(t)

                wait(m_ref.at[0:ROWS], sem.at[k])
                rows = pl.ds(pl.multiple_of(k * ROWS, ROWS), ROWS)
                j = 2 * k + half
                kinds = idx_r[half, k, 8 + lv : 9 + lv, :]
                factors = coefficients(m_ref[rows], kinds, j * ROWS, live[lv, mine])
                for i, f in enumerate(factors):
                    coef[lv, i, rows] = f
                xts[lv, :, rows] = kinds_ext(kinds)

            each(8, step)

        forward(0, m0, m0_sem)
        late()

        def relay(t):
            k = turn(t)
            rows = pl.ds(pl.multiple_of(half * OWN + k * ROWS, ROWS), ROWS)

            wait(d1.at[0:ROWS], dm_sem.at[k])
            send(d1.at[rows], d1.at[rows], sem_s.at[6], fw_sem, gate=sibling)

        each(8, relay)
        each(8, lambda i: wait(sg0.at[0:ROWS], sg0_sem.at[i]))
        wait(d1.at[0:OWN], fw_sem)

        def chunk(n):
            return pl.ds(pl.multiple_of(n * CHUNK, CHUNK), CHUNK)

        def backward(lv, s, n, dst, sem, ssem):
            rows = chunk(n)
            factors = tuple(coef[lv, i, rows] for i in range(5))
            dr, dz, dc, dn, down = grads(s, factors)
            for i, g in enumerate((dr, dz, dc, dn)):
                gbuf[rows, i * H : (i + 1) * H] = g
            place = pl.ds(pl.multiple_of(half * OWN + n * CHUNK, CHUNK), CHUNK)
            dst[place] = down
            send(dst.at[place], dst.at[place], ssem, sem, gate=sibling)

        def collect(lv, n, src):
            return dot_nn(sel[lv, chunk(n)], src[...])

        @pl.when(band > 0)
        def _():
            pl.semaphore_wait(below_ready, 1)

        def first_zero(n):
            s = sg0[chunk(n)].astype(F32) + collect(1, n, d1)
            s0[chunk(n)] = s
            backward(0, s, n, d2, ex_sem.at[0], sem_s.at[7])

        each(NCH, first_zero)
        wait(d2.at[0:OWN], ex_sem.at[0])

        def first_out(n):
            rows = chunk(n)
            q_s[rows] = collect(0, n, d2).astype(BF16)

            @pl.when(band > 0)
            def _():
                def part(e):
                    i = n * (CHUNK // PART) + e
                    place = pl.ds(pl.multiple_of(i * PART, PART), PART)

                    @pl.when(i < DETOUR // PART)
                    def _():
                        send(
                            q_s.at[place],
                            q_r.at[place],
                            sem_s.at[8],
                            qp_sem.at[i],
                            gate=2 * (2 * mine + 1 - parity) + half,
                        )

                    @pl.when(i >= DETOUR // PART)
                    def _():
                        send(
                            q_s.at[place],
                            q_r.at[place],
                            sem_s.at[8],
                            q_sem.at[n],
                            gate=2 * (2 * mine + below_parity) + half,
                            to_band=below,
                        )

                each(CHUNK // PART, part)

            @pl.when(band == bands - 1)
            def _():
                q_r[rows] = jnp.zeros((CHUNK, H), BF16)

        each(NCH, first_out)
        forward(1, m1, m1_sem)

        def second_one(n):
            @pl.when(band < bands - 1)
            def _():
                wait(q_r.at[0:CHUNK], q_sem.at[n])

            backward(1, q_r[chunk(n)].astype(F32), n, d3, ex_sem.at[1], sem_s.at[9])

        each(NCH, second_one)

        for i in range(3):
            wacc[:, i * H : (i + 1) * H] += dot_tn(m1[...], gbuf[:, i * H : (i + 1) * H])
        for i in range(4):
            eacc[:, i * H : (i + 1) * H] += dot_nn(xts[1], gbuf[:, i * H : (i + 1) * H])
        wait(d3.at[0:OWN], ex_sem.at[1])

        def second_zero(n):
            s = s0[chunk(n)] + collect(1, n, d3)
            backward(0, s, n, d4, ex_sem.at[2], sem_s.at[10])

        each(NCH, second_zero)
        for i in range(3):
            wacc[:, i * H : (i + 1) * H] += dot_tn(m0[...], gbuf[:, i * H : (i + 1) * H])
        for i in range(4):
            eacc[:, i * H : (i + 1) * H] += dot_nn(xts[0], gbuf[:, i * H : (i + 1) * H])
        halve()

        wait(d4.at[0:OWN], ex_sem.at[2])

        @pl.when(band > 0)
        def _():
            wait(q_s, sem_s.at[8])

        def second_out(n):
            q_s[chunk(n)] = collect(0, n, d4).astype(BF16)

        def deliver(k):
            @pl.when(k == z)
            def _():
                out[mine] = q_s[block(k)]

            @pl.when(k != z)
            def _():
                send(q_s.at[block(k)], out.at[mine], sem_s.at[12], out_sem, gate=2 * k + half)

        over_plane()
        each(NCH // 2, second_out)
        each(NCH // 2, lambda n: second_out(NCH // 2 + n))
        along_ring()
        each(8, deliver)

    @pl.when(jnp.logical_not(active))
    def _():
        for _, buf, base, ssem, rsem in first_units:
            hand_on(buf, base, ssem, rsem)
        for i in range(1, 4):
            wait(m0.at[0 : 4 * ROWS + PASSED], sem_s.at[i])
        late()
        hand_on(*last_unit[1:])

        @pl.when(band > 0)
        def _():
            def pass_on(i):
                place = pl.ds(pl.multiple_of(i * PART, PART), PART)
                wait(q_r.at[0:PART], qp_sem.at[i])
                send(
                    q_r.at[place],
                    q_r.at[place],
                    sem_s.at[8],
                    q_sem.at[i // (CHUNK // PART)],
                    gate=2 * (2 * mine + below_parity) + half,
                    to_band=below,
                )

            pl.semaphore_wait(below_ready, 1)
            each(DETOUR // PART, pass_on)

        halve()
        over_plane()
        along_ring()

    wait(z_r.at[0:7], wr_sem.at[4])
    total = z_r[0].astype(F32)
    for i in range(1, 8):
        total = total + z_r[i].astype(F32)
    total = total * (1.0 / math.sqrt(CIRC * bands * 2 * ROWS * GATES))
    done = piece_of(summed.at[half], place)
    done[...] = total.astype(BF16)

    def to_plane(i):
        peer = lax.rem(place + 1 + i, bands)
        send_in_plane(done, done, sem_s.at[16], ax_sem.at[bx], peer)

    each(bands - 1, to_plane)

    def to_sibling(i):
        x = lax.rem(bx + i, rows_x)
        there = x_part(summed.at[half], x)

        @pl.when(i == 0)
        def _():
            wait(plane_r.at[0 : rows_y - 1], ax_sem.at[x])

        @pl.when(i > 0)
        def _():
            wait(plane_r.at[0:rows_y], ax_sem.at[x])

        send(there, there, sem_s.at[17], wr_sem.at[6], gate=sibling)

    each(rows_x, to_sibling)
    wait(summed.at[half], wr_sem.at[6])

    @pl.when(active)
    def _():
        wait(out.at[0:3], out_sem)
        wait(idx_r.at[0, 0:3], sem_s.at[0])
        wait(idx_r.at[0], sem_s.at[18])
        for i in range(1, 5):
            wait(m0.at[0 : 3 * ROWS], sem_s.at[i])
        wait(d1.at[0:OWN], sem_s.at[6])
        wait(d1.at[0:OWN], sem_s.at[7])
        wait(d1.at[0:OWN], sem_s.at[9])
        wait(d1.at[0:OWN], sem_s.at[10])
        wait(q_s.at[0 : 7 * ROWS], sem_s.at[12])

    @pl.when(jnp.logical_not(active))
    def _():
        wait(out, out_sem)
        wait(idx_r.at[0, 0:4], sem_s.at[0])
        wait(m0.at[0 : 4 * ROWS + PASSED], sem_s.at[4])

        @pl.when(band > 0)
        def _():
            wait(q_r.at[0:DETOUR], sem_s.at[8])

    wait(half_r, sem_s.at[5])
    wait(plane_r.at[0 : bands - 1], sem_s.at[11])
    wait(z_r.at[0:7], sem_s.at[15])
    wait(plane_r.at[0 : bands - 1], sem_s.at[16])
    wait(summed.at[half], sem_s.at[17])


def finish_body(moved, summed, out, wout, bout, tout):
    out[...] = moved[...]
    for s in range(GATES):
        for n in range(3):
            wout[16 * s : 16 * s + 16, n * H : (n + 1) * H] = summed[s % 2, n, s // 2].astype(F32)
    for s in range(4):
        ext = summed[s % 2, 3, s // 2].astype(F32)
        if s != 2:
            n = min(s, 2)
            tout[:, n * H : (n + 1) * H] = ext[:8]
        if s < 3:
            bout[s * H : (s + 1) * H] = ext[8]


def shards(
    messages,
    gate_type,
    state_grad,
    fanin_owner,
    fanin_slot,
    live_count,
    hidden_weight,
    hidden_bias,
    type_table,
):
    bands = lax.axis_size("band")
    cols = min(8, bands)
    rows_x = bands // cols
    py, px = 8 // cols, 4 // rows_x
    owners = jnp.swapaxes(fanin_owner[:, 0], 2, 3)
    slots = jnp.swapaxes(fanin_slot[:, 0], 2, 3)
    vmem = pl.BlockSpec(memory_space=pltpu.VMEM)
    hbm = pl.BlockSpec(memory_space=pl.ANY)
    dma = pltpu.SemaphoreType.DMA

    def body(*refs):
        kernel_body(bands, cols, *refs)

    moved, summed = pl.pallas_call(
        body,
        out_shape=(
            jax.ShapeDtypeStruct((CIRC, ROWS, H), BF16),
            jax.ShapeDtypeStruct((2,) + PIECES, BF16),
        ),
        in_specs=[hbm, vmem, hbm, vmem, vmem, pl.BlockSpec(memory_space=pltpu.SMEM)] + [vmem] * 3,
        out_specs=(vmem, vmem),
        scratch_shapes=[
            pltpu.VMEM((CIRC, 16, ROWS), jnp.int32),
            pltpu.VMEM((2, 8, 16, ROWS), jnp.int32),
            pltpu.VMEM((32, 3 * H), BF16),
            pltpu.VMEM((OWN, H), BF16),
            pltpu.VMEM((OWN, H), BF16),
            pltpu.VMEM((OWN, H), BF16),
            pltpu.VMEM((CIRC, ROWS, H), BF16),
            pltpu.VMEM((2 * OWN, H), BF16),
            pltpu.VMEM((2 * OWN, H), BF16),
            pltpu.VMEM((2 * OWN, H), BF16),
            pltpu.VMEM((2 * OWN, H), BF16),
            pltpu.VMEM((2, OWN, 2 * OWN), BF16),
            pltpu.VMEM((2, 5, OWN, H), F32),
            pltpu.VMEM((2, 16, OWN), BF16),
            pltpu.VMEM((OWN, H), F32),
            pltpu.VMEM((OWN, 4 * H), BF16),
            pltpu.VMEM((OWN, H), BF16),
            pltpu.VMEM((OWN, H), BF16),
            pltpu.VMEM((H, 3 * H), F32),
            pltpu.VMEM((16, 4 * H), F32),
            pltpu.VMEM((CIRC, ROWS, H), BF16),
            pltpu.VMEM((CIRC, ROWS, H), BF16),
            pltpu.VMEM((2,) + PIECES, BF16),
            pltpu.VMEM(PIECES, BF16),
            pltpu.VMEM(PIECES, BF16),
            pltpu.VMEM((bands, px, py, 16, H), BF16),
            pltpu.VMEM((8, px, py, 16, H), BF16),
            dma((19,)),
            dma,
            dma,
            dma((8,)),
            dma((8,)),
            dma((8,)),
            dma((8,)),
            dma,
            dma((3,)),
            dma((NCH,)),
            dma((DETOUR // PART,)),
            dma,
            dma((7,)),
            dma((rows_x,)),
            dma((2,)),
            pltpu.SemaphoreType.REGULAR,
            pltpu.SemaphoreType.REGULAR,
            pltpu.SemaphoreType.REGULAR,
        ],
        compiler_params=pltpu.CompilerParams(
            collective_id=0, has_side_effects=True, vmem_limit_bytes=56 * 1024 * 1024
        ),
        name="band_passes",
    )(
        messages[:, 0],
        gate_type[:, 0],
        state_grad[:, 0],
        owners,
        slots,
        live_count[:, 0].T,
        hidden_weight,
        hidden_bias,
        type_table,
    )
    out, weight, bias, rows = pl.pallas_call(
        finish_body,
        out_shape=(
            jax.ShapeDtypeStruct((CIRC, ROWS, H), BF16),
            jax.ShapeDtypeStruct((H, 3 * H), F32),
            jax.ShapeDtypeStruct((3 * H,), F32),
            jax.ShapeDtypeStruct((8, 3 * H), F32),
        ),
        in_specs=[vmem] * 2,
        out_specs=(vmem,) * 4,
        name="results",
    )(moved, summed)
    return out[:, None], weight, bias, rows


def solution(mesh):
    return jax.shard_map(
        shards,
        mesh=mesh,
        in_specs=(
            P(None, "band", None, "gate", None),
            P(None, "band", None, "gate"),
            P(None, "band", None, "gate", None),
            P(None, "band", None, "gate", None),
            P(None, "band", None, "gate", None),
            P(None, "band", None),
            P(),
            P(),
            P(),
        ),
        out_specs=(P(None, "band", "gate", None), P(), P(), P()),
        check_vma=False,
    )
```
